32 devices in a mesh: seq: 8 (over y, x, core), head: 4 (over z).
Axes of the slice: x: 2, y: 2, z: 4, core: 2. Of those that a mesh axis runs over, the one named last changes fastest.
Arguments:
- query_rows: bfloat16 [4096, 1024], P('seq', 'head'), may hold values from -100 to 100
- key_rows: bfloat16 [4096, 1024], P('seq', 'head'), may hold values from -4 to 4
- value_rows: bfloat16 [4096, 1024], P('seq', 'head'), may hold values from -6 to 6
- out_grad: bfloat16 [4096, 1024], P('seq', 'head'), may hold values from -6 to 6
- members: int32 [4096], P(('seq', 'head')), may hold values from 0 to 4095, as said below
Outputs:
- attn_out: bfloat16 [4096, 1024], P('seq', 'head')
- query_grad: bfloat16 [4096, 1024], P('seq', 'head')
- key_grad: bfloat16 [4096, 1024], P('seq', 'head')
- value_grad: bfloat16 [4096, 1024], P('seq', 'head')
The draws below stay inside these ranges and needn't reach their ends.
Inputs may be any that keep to these rules, and one draw needn't show every extreme that they name: `members`: every position appears once; the 512 positions of each cluster stand in ascending order. Of the 512 positions of one index of seq a cluster takes 0, 64 or 128, and for each index of seq some clusters take 128. The positions may be sent packed, several to a 32-bit word, or in any narrower integer form that holds them exactly.
All inputs are finite; a program needn't handle non-finite values.
Results may differ from the reference program's by a relative error of at most 0.008.
Values may be sent and summed in bfloat16 or wider, within the bound.
No kernel may reach another device: no remote copies, remote signals or barrier semaphores. Data moves between devices by JAX's collectives and lax.ppermute only.
A program may use at most 64 MiB of HBM per device.

```python
import math
import jax
import jax.numpy as jnp
from jax import lax

HD = 128
CLUS = 512
WINDOW = 512
TOK_DEV = 512
SEQ = 4096
HEADS = 8


def cluster_layout(base):
    shards = SEQ // TOK_DEV
    clusters = SEQ // CLUS
    per_dev = clusters // shards
    per_pair = CLUS // shards
    perm_keys = jax.random.split(jax.random.fold_in(base, 11), per_dev)

    def one_order(order_key):
        return jax.random.permutation(order_key, shards)
    orders = jax.vmap(one_order)(perm_keys)
    following = jnp.roll(orders, -1, axis=1)
    owners = jnp.arange(shards)
    high_mark = (owners[None, None, :] == orders[:, :, None]).astype(jnp.int32)
    low_mark = (owners[None, None, :] == following[:, :, None]).astype(jnp.int32)
    counts = per_pair * (1 + high_mark - low_mark)
    counts = jnp.transpose(counts, (1, 2, 0)).reshape(shards, clusters)
    bounds = jnp.cumsum(counts, axis=1)
    positions = jnp.arange(TOK_DEV)
    labels = jnp.sum((bounds[:, None, :] <= positions[None, :, None]).astype(jnp.int32), axis=2)
    shuffle_keys = jax.random.split(jax.random.fold_in(base, 12), shards)

    def shuffled(shuffle_key, label_row):
        return jax.random.permutation(shuffle_key, label_row)
    labels = jax.vmap(shuffled)(shuffle_keys, labels)
    return jnp.argsort(labels.reshape(-1), stable=True).astype(jnp.int32)


def drawn_pair(base):
    heads = HEADS
    shape = (SEQ, heads, HD)
    key_final = jnp.clip(jax.random.normal(jax.random.fold_in(base, 21), shape, jnp.float32), -4.0, 4.0)
    query_final = jnp.clip(jax.random.normal(jax.random.fold_in(base, 23), shape, jnp.float32), -4.0, 4.0)
    return (key_final.reshape(SEQ, heads * HD), query_final.reshape(SEQ, heads * HD))


def draw_members(key, part):
    return cluster_layout(key)


def draw_key_rows(key, part):
    return drawn_pair(key)[0].astype(jnp.bfloat16)


def draw_query_rows(key, part):
    return drawn_pair(key)[1].astype(jnp.bfloat16)


def levels(own_key, dims, cuts, least, top_value):
    level, own = 1.0, jax.random.fold_in(own_key, 6)
    for dim, shards_of in cuts:
        draws = jnp.exp(jax.random.uniform(jax.random.fold_in(own, dim), (shards_of,), jnp.float32, least / len(cuts), top_value / len(cuts)))
        level = level * jnp.repeat(draws, dims[dim] // shards_of).reshape([-1 if axis == dim else 1 for axis in range(len(dims))])
    return level


def scatter_about(stream_key, shape, width, reach, pieces=(), kind=jnp.bfloat16):
    values = jax.random.normal(stream_key, shape, jnp.float32) * width
    if len(pieces) > 0:
        values = levels(stream_key, shape, pieces, -0.22, 0.18) * values
    return jnp.clip(values, min=-reach, max=reach).astype(kind)


def setup_inputs(seed: int = 0) -> dict:
    splits = jax.random.split(jax.random.key(seed), 6)
    return {
        "query_rows": draw_query_rows(jax.random.fold_in(splits[5], 71), 0),
        "key_rows": draw_key_rows(jax.random.fold_in(splits[5], 71), 0),
        "value_rows": scatter_about(splits[2], (SEQ, HEADS * HD), 1.0, 6.0, ((0, 8), (1, 4))),
        "out_grad": scatter_about(splits[3], (SEQ, HEADS * HD), 1.0, 6.0, ((0, 8), (1, 4))),
        "members": draw_members(jax.random.fold_in(splits[5], 71), 0),
    }


def weighted_product(form, left, right):
    return jnp.einsum(form, left.astype(jnp.float32), right.astype(jnp.float32), precision=lax.Precision.HIGHEST)

def attend(query_matrix, input_keys, value_matrix, upstream_gradient, allowed):
    logit_scale = 1.0 / math.sqrt(query_matrix.shape[-1])
    attention_scores = weighted_product('vnw,vtw->vnt', query_matrix, input_keys) * logit_scale
    attention_scores = jnp.where(allowed, attention_scores, -jnp.inf)
    row_max = lax.optimization_barrier(jnp.max(attention_scores, axis=-1, keepdims=True))
    exp_scores = jnp.exp(attention_scores - row_max)
    probability = exp_scores / lax.optimization_barrier(jnp.sum(exp_scores, axis=-1, keepdims=True))
    attention_weights = lax.optimization_barrier(probability.astype(jnp.bfloat16))
    attended_output = weighted_product('yxs,ysl->yxl', attention_weights, value_matrix)
    probability_gradient = weighted_product('vnw,vtw->vnt', upstream_gradient, value_matrix)
    row_delta = lax.optimization_barrier(jnp.sum(probability * probability_gradient, axis=-1, keepdims=True))
    score_gradient = lax.optimization_barrier((probability * (probability_gradient - row_delta) * logit_scale).astype(jnp.bfloat16))
    query_gradient = weighted_product('yxs,ysl->yxl', score_gradient, input_keys)
    key_gradient = weighted_product('ipy,ipg->iyg', score_gradient, query_matrix)
    value_gradient = weighted_product('ipy,ipg->iyg', attention_weights, upstream_gradient)
    return (attended_output, query_gradient, key_gradient, value_gradient)

def window_head(query_matrix, input_keys, value_matrix, upstream_gradient):
    seq_len = query_matrix.shape[0]
    window_len = WINDOW
    blocks = seq_len // window_len
    padding = jnp.zeros((window_len, query_matrix.shape[1]), query_matrix.dtype)
    extended_keys = jnp.concatenate([padding, input_keys], axis=0)
    extended_values = jnp.concatenate([padding, value_matrix], axis=0)

    def framed(extended):
        return jnp.concatenate([extended[:seq_len].reshape(blocks, window_len, -1), extended[window_len:].reshape(blocks, window_len, -1)], axis=1)

    def unframe(blockwise):
        lower_half = blockwise[:, :window_len].reshape(seq_len, -1)
        upper_half = blockwise[:, window_len:].reshape(seq_len, -1)
        return jnp.pad(lower_half, ((0, window_len), (0, 0))) + jnp.pad(upper_half, ((window_len, 0), (0, 0)))
    query_pos = jnp.arange(window_len)[None, :, None]
    key_pos = jnp.arange(2 * window_len)[None, None, :]
    block_pos = jnp.arange(blocks)[:, None, None]
    allowed = (key_pos > query_pos) & (key_pos <= query_pos + window_len) & (block_pos * window_len + key_pos >= window_len)
    attended_output, query_gradient, key_gradient, value_gradient = attend(query_matrix.reshape(blocks, window_len, -1), framed(extended_keys), framed(extended_values), upstream_gradient.reshape(blocks, window_len, -1), allowed)
    return (attended_output.reshape(seq_len, -1).astype(jnp.bfloat16), query_gradient.reshape(seq_len, -1).astype(jnp.bfloat16), unframe(key_gradient)[window_len:].astype(jnp.bfloat16), unframe(value_gradient)[window_len:].astype(jnp.bfloat16))

def reference(query_rows, key_rows, value_rows, out_grad, members):
    seq_len = query_rows.shape[0]
    heads_half = query_rows.shape[1] // (2 * HD)

    def split_heads(array):
        return array.reshape(seq_len, heads_half, 2, HD)

    def window_slice(array):
        return jnp.transpose(split_heads(array)[:, :, 0], (1, 0, 2))

    def cluster_slice(array):
        return split_heads(array)[:, :, 1]

    def window_pack(packed):
        return window_head(packed[0], packed[1], packed[2], packed[3])
    window_results = lax.map(window_pack, (window_slice(query_rows), window_slice(key_rows), window_slice(value_rows), window_slice(out_grad)))
    window_stack = jnp.stack([jnp.transpose(result, (1, 0, 2)) for result in window_results])
    route_query = cluster_slice(query_rows)
    route_key = cluster_slice(key_rows)
    route_value = cluster_slice(value_rows)
    route_grad = cluster_slice(out_grad)
    member_table = members.reshape(-1, CLUS)
    causal = (jnp.arange(CLUS)[:, None] >= jnp.arange(CLUS)[None, :])[None]

    def one_cluster(indices):
        group_query = jnp.transpose(route_query[indices], (1, 0, 2))
        group_key = jnp.transpose(route_key[indices], (1, 0, 2))
        group_value = jnp.transpose(route_value[indices], (1, 0, 2))
        group_grad = jnp.transpose(route_grad[indices], (1, 0, 2))
        results = attend(group_query, group_key, group_value, group_grad, causal)
        return jnp.stack(results).astype(jnp.bfloat16)
    gathered = lax.map(one_cluster, member_table)
    ordered = jnp.transpose(gathered, (1, 0, 3, 2, 4)).reshape(4, seq_len, heads_half, HD)
    placed = jnp.zeros_like(ordered).at[:, members].set(ordered)
    combined = jnp.stack([window_stack, placed], axis=3).reshape(4, seq_len, heads_half * 2 * HD)
    return (combined[0], combined[1], combined[2], combined[3])
```

```python
import functools
import math

import jax
import jax.numpy as jnp
from jax import lax
from jax.experimental import pallas as pl
from jax.experimental.pallas import tpu as pltpu
from jax.sharding import PartitionSpec as P

CLUS = 512
WINDOW = 512
F32 = jnp.float32
BF16 = jnp.bfloat16
NEG = -1e30
VMEM_LIMIT = 60 * 1024 * 1024

NN = (((1,), (0,)), ((), ()))
NT = (((1,), (1,)), ((), ()))
TN = (((0,), (0,)), ((), ()))


def dot(left, right, dims=NN):
    return lax.dot_general(left, right, dims, preferred_element_type=F32)


def call(body, outs, inputs, scratch=(), smem=(), flops=0, smem_outs=()):
    in_specs = [
        pl.BlockSpec(memory_space=pltpu.SMEM if i in smem else pltpu.VMEM)
        for i in range(len(inputs))
    ]
    out_specs = [
        pl.BlockSpec(memory_space=pltpu.SMEM if i in smem_outs else pltpu.VMEM)
        for i in range(len(outs))
    ]
    moved = sum(x.size * x.dtype.itemsize for x in list(inputs) + list(outs))
    return pl.pallas_call(
        body,
        out_shape=outs,
        in_specs=in_specs,
        out_specs=out_specs,
        scratch_shapes=list(scratch),
        compiler_params=pltpu.CompilerParams(vmem_limit_bytes=VMEM_LIMIT),
        cost_estimate=pl.CostEstimate(flops=flops, bytes_accessed=moved, transcendentals=0),
    )(*inputs)


def shape(*dims, dtype=BF16):
    return jax.ShapeDtypeStruct(dims, dtype)


def to_row(column):
    n = column.shape[0]
    same = lax.broadcasted_iota(jnp.int32, (n, n), 0) == lax.broadcasted_iota(jnp.int32, (n, n), 1)
    return jnp.sum(jnp.where(same, column, 0.0), axis=0, keepdims=True)


def window_queries(tok, hd, tile, me_ref, q_ref, k_ref, v_ref, g_ref, halo_ref, out_ref, dq_ref, st_ref, kx, vx):
    scale = 1.0 / math.sqrt(hd)
    kx[0:tok] = halo_ref[:, 0:hd]
    kx[tok:] = k_ref[:, 0:hd]
    vx[0:tok] = halo_ref[:, hd:]
    vx[tok:] = v_ref[:, 0:hd]
    first = jnp.where(me_ref[0] == 0, tok, 0)
    span = tok + tile
    row = lax.broadcasted_iota(jnp.int32, (tile, span), 0)
    col = lax.broadcasted_iota(jnp.int32, (tile, span), 1)
    st_ref[...] = jnp.zeros_like(st_ref)
    for r in range(tok // tile):
        lo = r * tile
        q = q_ref[lo : lo + tile, 0:hd]
        g = g_ref[lo : lo + tile, 0:hd]
        keys = kx[lo : lo + span]
        values = vx[lo : lo + span]
        allowed = (col > row) & (col <= row + tok) & (col + lo >= first)
        s = jnp.where(allowed, dot(q, keys, NT) * scale, NEG)
        top = jnp.max(s, axis=1, keepdims=True)
        e = jnp.exp(s - top)
        total = jnp.sum(e, axis=1, keepdims=True)
        p = e * (1.0 / total)
        out_ref[lo : lo + tile] = dot(p.astype(BF16), values).astype(BF16)
        dp = dot(g, values, NT)
        delta = jnp.sum(p * dp, axis=1, keepdims=True)
        ds = (p * (dp - delta) * scale).astype(BF16)
        dq_ref[lo : lo + tile] = dot(ds, keys).astype(BF16)
        st_ref[0:1, lo : lo + tile] = to_row(top + jnp.log(total))
        st_ref[1:2, lo : lo + tile] = to_row(delta)


def window_keys(tok, hd, tile, me_ref, q_ref, k_ref, v_ref, g_ref, halo_ref, st_ref, stn_ref, dk_ref, dv_ref, qx, gx):
    scale = 1.0 / math.sqrt(hd)
    qx[0:tok] = q_ref[:, 0:hd]
    qx[tok:] = halo_ref[:, 0:hd]
    gx[0:tok] = g_ref[:, 0:hd]
    gx[tok:] = halo_ref[:, hd:]
    last = jnp.where(me_ref[1] == 1, tok, 2 * tok)
    span = tok + tile
    row = lax.broadcasted_iota(jnp.int32, (tile, span), 0)
    col = lax.broadcasted_iota(jnp.int32, (tile, span), 1)
    for r in range(tok // tile):
        lo = r * tile
        k = k_ref[lo : lo + tile, 0:hd]
        v = v_ref[lo : lo + tile, 0:hd]
        queries = qx[lo : lo + span]
        grads = gx[lo : lo + span]
        stats = jnp.concatenate([st_ref[0:2, lo:], stn_ref[0:2, 0 : lo + tile]], axis=1)
        allowed = (col >= row) & (col < row + tok) & (col + lo < last)
        s = dot(k, queries, NT) * scale
        p = jnp.where(allowed, jnp.exp(jnp.where(allowed, s - stats[0:1], NEG)), 0.0)
        dv_ref[lo : lo + tile] = dot(p.astype(BF16), grads).astype(BF16)
        dp = dot(v, grads, NT)
        ds = (jnp.where(allowed, p * (dp - stats[1:2]), 0.0) * scale).astype(BF16)
        dk_ref[lo : lo + tile] = dot(ds, queries).astype(BF16)


def list_row(m, cfg, me_seq, me_head):
    row = m // cfg["per_row"]
    seq = row // cfg["heads"]
    head = row % cfg["heads"]
    mask = seq ^ me_seq
    at = (mask % 2) * (cfg["shards"] // 2 * cfg["heads"]) + (mask // 2) * cfg["heads"] + (head ^ me_head)
    return at, m % cfg["per_row"]


def make_tables(cfg, me_ref, lists_smem, src_tab, pos_tab, chunk_tab, count):
    shards, g, tok = cfg["shards"], cfg["g"], cfg["tok"]
    me_seq, me_head = me_ref[0], me_ref[2]
    for s in range(shards):
        count[s] = 0

    def step(m, carry):
        at, half = list_row(m, cfg, me_seq, me_head)
        s = lists_smem[at, half * g] // tok
        pos = count[s]
        count[s] = pos + 1
        src_tab[m] = s
        pos_tab[m] = pos
        chunk_tab[s * shards + pos] = m
        return carry

    lax.fori_loop(0, cfg["chunks"], step, 0)


def build_order(cfg, me_ref, lists_ref, chunk_tab, s, order_ref):
    shards, g, tok, per = cfg["shards"], cfg["g"], cfg["tok"], cfg["per"]
    sub = lax.broadcasted_iota(jnp.int32, (g, per), 0)
    lane = lax.broadcasted_iota(jnp.int32, (g, per), 1)
    token = lax.broadcasted_iota(jnp.int32, (g, tok), 1)

    def step(k, carry):
        m = chunk_tab[s * shards + k]
        at, half = list_row(m, cfg, me_ref[0], me_ref[2])
        row = lists_ref[pl.ds(at, 1), :] - s * tok
        picked = jnp.where(lane == sub + half * g, row, 0).astype(F32)
        column = jnp.sum(picked, axis=1, keepdims=True).astype(jnp.int32)
        order_ref[pl.ds(pl.multiple_of(k * g, g), g), :] = jnp.where(column == token, 1.0, 0.0).astype(BF16)
        return carry

    lax.fori_loop(0, shards, step, 0, unroll=min(shards, 8))


def place(cfg, chunk_tab, s, rows_ref, to_ref):
    shards, g = cfg["shards"], cfg["g"]

    def step(k, carry):
        m = chunk_tab[s * shards + k]
        to_ref[pl.ds(pl.multiple_of(m * g, g), g), :] = rows_ref[pl.ds(pl.multiple_of(k * g, g), g), :]
        return carry

    lax.fori_loop(0, shards, step, 0, unroll=min(shards, 8))


def cluster_queries(cfg, *refs):
    shards, g, tok, hd = cfg["shards"], cfg["g"], cfg["tok"], cfg["hd"]
    (me_ref, lists_smem, lists_ref, q_ref, k_ref, v_ref, g_ref, ow_ref, dqw_ref), refs = refs[:9], refs[9:]
    arrived, refs = refs[: shards - 1], refs[shards - 1 :]
    out_ref, dq_ref, st_ref, rows_ref, kv_ref, order_ref, src_tab, pos_tab, chunk_tab = refs[:9]
    count, order, sorted_rows, qg, stats, outs = refs[9:]
    scale = 1.0 / math.sqrt(hd)
    me = me_ref[0]
    make_tables(cfg, me_ref, lists_smem, src_tab, pos_tab, chunk_tab, count)
    build_order(cfg, me_ref, lists_ref, chunk_tab, me, order_ref)
    own_order = order_ref[...]
    qg[:, 0:hd] = dot(own_order, q_ref[:, hd:]).astype(BF16)
    qg[:, hd:] = dot(own_order, g_ref[:, hd:]).astype(BF16)
    kv_ref[:, 0:hd] = dot(own_order, k_ref[:, hd:]).astype(BF16)
    kv_ref[:, hd:] = dot(own_order, v_ref[:, hd:]).astype(BF16)
    place(cfg, chunk_tab, me, kv_ref, rows_ref)
    for mask in range(1, shards):
        s = me ^ mask
        build_order(cfg, me_ref, lists_ref, chunk_tab, s, order)
        sorted_rows[...] = dot(order[...], arrived[mask - 1][...]).astype(BF16)
        place(cfg, chunk_tab, s, sorted_rows, rows_ref)
    key_at = lax.broadcasted_iota(jnp.int32, (g, CLUS), 1)
    query_at = lax.broadcasted_iota(jnp.int32, (g, CLUS), 0)

    def step(k, carry):
        m = chunk_tab[me * shards + k]
        cluster = m // shards
        rank = (m % shards) * g
        mine = pl.ds(pl.multiple_of(k * g, g), g)
        whole = pl.ds(pl.multiple_of(cluster * CLUS, CLUS), CLUS)
        q = qg[mine, 0:hd]
        gr = qg[mine, hd:]
        keys = rows_ref[whole, 0:hd]
        values = rows_ref[whole, hd:]
        s = jnp.where(key_at <= query_at + rank, dot(q, keys, NT) * scale, NEG)
        top = jnp.max(s, axis=1, keepdims=True)
        e = jnp.exp(s - top)
        total = jnp.sum(e, axis=1, keepdims=True)
        p = e * (1.0 / total)
        outs[mine, 0:hd] = dot(p.astype(BF16), values).astype(BF16)
        dp = dot(gr, values, NT)
        delta = jnp.sum(p * dp, axis=1, keepdims=True)
        ds = (p * (dp - delta) * scale).astype(BF16)
        outs[mine, hd:] = dot(ds, keys).astype(BF16)
        stats[mine, 0:1] = top + jnp.log(total)
        stats[mine, 1:2] = delta
        return carry

    lax.fori_loop(0, shards, step, 0, unroll=min(shards, 4))
    back = dot(own_order, outs[...], TN).astype(BF16)
    out_ref[:, 0:hd] = ow_ref[...]
    out_ref[:, hd:] = back[:, 0:hd]
    dq_ref[:, 0:hd] = dqw_ref[...]
    dq_ref[:, hd:] = back[:, hd:]
    st_ref[...] = jnp.zeros_like(st_ref)
    for lo in range(0, tok, 128):
        st_ref[0:1, lo : lo + 128] = to_row(stats[lo : lo + 128, 0:1])
        st_ref[1:2, lo : lo + 128] = to_row(stats[lo : lo + 128, 1:2])
    place(cfg, chunk_tab, me, qg, rows_ref)


def cluster_keys(cfg, *refs):
    shards, g, tok, hd = cfg["shards"], cfg["g"], cfg["tok"], cfg["hd"]
    (me_ref, src_tab, pos_tab, chunk_tab, rows_ref, kv_ref, order_ref, dkw_ref, dvw_ref, st_ref), refs = refs[:10], refs[10:]
    arrived, refs = refs[: shards - 1], refs[shards - 1 :]
    dk_ref, dv_ref, columns, stats, outs = refs
    scale = 1.0 / math.sqrt(hd)
    me = me_ref[0]
    for mask in range(shards):
        s = me ^ mask
        st = st_ref if mask == 0 else arrived[mask - 1]
        columns[:, 0:8] = jnp.transpose(st[...])
        place(cfg, chunk_tab, s, columns, stats)
    query_at = lax.broadcasted_iota(jnp.int32, (CLUS, g), 0)
    key_at = lax.broadcasted_iota(jnp.int32, (CLUS, g), 1)

    def step(k, carry):
        m = chunk_tab[me * shards + k]
        cluster = m // shards
        rank = (m % shards) * g
        mine = pl.ds(pl.multiple_of(k * g, g), g)
        whole = pl.ds(pl.multiple_of(cluster * CLUS, CLUS), CLUS)
        keys = kv_ref[mine, 0:hd]
        values = kv_ref[mine, hd:]
        queries = rows_ref[whole, 0:hd]
        grads = rows_ref[whole, hd:]
        allowed = query_at >= key_at + rank
        s = dot(queries, keys, NT) * scale
        p = jnp.where(allowed, jnp.exp(jnp.where(allowed, s - stats[whole, 0:1], NEG)), 0.0)
        dp = dot(grads, values, NT)
        ds = (jnp.where(allowed, p * (dp - stats[whole, 1:2]), 0.0) * scale).astype(BF16)
        outs[mine, 0:hd] = dot(ds, queries, TN).astype(BF16)
        outs[mine, hd:] = dot(p.astype(BF16), grads, TN).astype(BF16)
        return carry

    lax.fori_loop(0, shards, step, 0, unroll=min(shards, 4))
    back = dot(order_ref[...], outs[...], TN).astype(BF16)
    dk_ref[:, 0:hd] = dkw_ref[...]
    dk_ref[:, hd:] = back[:, 0:hd]
    dv_ref[:, 0:hd] = dvw_ref[...]
    dv_ref[:, hd:] = back[:, hd:]


def partner(array, axis, mask):
    size = lax.axis_size(axis)
    return lax.ppermute(array, axis, [(i, i ^ mask) for i in range(size)])


def all_partners(pieces, shards):
    got = {1: partner(pieces[0], "seq", 1)}
    for mask in range(2, shards, 2):
        got[mask] = partner(pieces[mask.bit_length() - 1], "seq", mask)
    for mask in range(2, shards, 2):
        got[mask + 1] = partner(got[mask], "seq", 1)
    return [got[mask] for mask in range(1, shards)]


def on_device(query_rows, key_rows, value_rows, out_grad, members):
    tok, width = query_rows.shape
    hd = width // 2
    shards = lax.axis_size("seq")
    heads = lax.axis_size("head")
    me = lax.axis_index("seq")
    per = members.shape[0]
    total = per * shards * heads
    g = CLUS // shards
    cfg = dict(
        shards=shards, heads=heads, tok=tok, hd=hd, per=per, g=g, chunks=total // g, per_row=per // g
    )
    place_ref = jnp.stack([me, (me == shards - 1).astype(jnp.int32), lax.axis_index("head")])

    lists = members.reshape(1, per)
    lists = jnp.concatenate([lists] + [partner(lists, "head", mask) for mask in range(1, heads)], axis=0)
    lists = jnp.concatenate([lists] + [partner(lists, "seq", mask) for mask in range(2, shards, 2)], axis=0)
    lists = jnp.concatenate([lists, partner(lists, "seq", 1)], axis=0)

    key_side = jnp.concatenate([key_rows[:, hd:], value_rows[:, hd:]], axis=1)
    query_side = jnp.concatenate([query_rows[:, hd:], out_grad[:, hd:]], axis=1)
    pieces = [
        jnp.where((me >> bit) % 2 == 0, key_side, query_side) for bit in range(shards.bit_length() - 1)
    ]
    arrived = all_partners(pieces, shards)
    before = lax.ppermute(
        jnp.concatenate([key_rows[:, :hd], value_rows[:, :hd]], axis=1),
        "seq",
        [(i, i + 1) for i in range(shards - 1)],
    )
    after = lax.ppermute(
        jnp.concatenate([query_rows[:, :hd], out_grad[:, :hd]], axis=1),
        "seq",
        [(i + 1, i) for i in range(shards - 1)],
    )

    tile = 128
    half = shape(tok, hd)
    full = shape(tok, width)
    stat = shape(8, tok, dtype=F32)
    wide = 6 * 2 * tok * (tok + tile) * hd
    out_w, dq_w, st_w = call(
        functools.partial(window_queries, tok, hd, tile),
        [half, half, stat],
        [place_ref, query_rows, key_rows, value_rows, out_grad, before],
        scratch=[pltpu.VMEM((2 * tok, hd), BF16)] * 2,
        smem=(0,),
        flops=wide,
    )
    st_next = lax.ppermute(st_w, "seq", [(i + 1, i) for i in range(shards - 1)])
    table = shape(total // g, dtype=jnp.int32)
    attn_out, query_grad, st_c, rows, kv, order, src, pos, chunk = call(
        functools.partial(cluster_queries, cfg),
        [full, full, stat, shape(total, 2 * hd), full, shape(tok, tok), table, table, table],
        [place_ref, lists, lists, query_rows, key_rows, value_rows, out_grad, out_w, dq_w] + arrived,
        scratch=[
            pltpu.SMEM((shards,), jnp.int32),
            pltpu.VMEM((tok, tok), BF16),
            pltpu.VMEM((tok, 2 * hd), BF16),
            pltpu.VMEM((tok, 2 * hd), BF16),
            pltpu.VMEM((tok, 128), F32),
            pltpu.VMEM((tok, 2 * hd), BF16),
        ],
        smem=(0, 1),
        smem_outs=(6, 7, 8),
        flops=wide * 2,
    )
    st_all = all_partners([st_c] * (shards.bit_length() - 1), shards)
    dk_w, dv_w = call(
        functools.partial(window_keys, tok, hd, tile),
        [half, half],
        [place_ref, query_rows, key_rows, value_rows, out_grad, after, st_w, st_next],
        scratch=[pltpu.VMEM((2 * tok, hd), BF16)] * 2,
        smem=(0,),
        flops=wide,
    )
    key_grad, value_grad = call(
        functools.partial(cluster_keys, cfg),
        [full, full],
        [place_ref, src, pos, chunk, rows, kv, order, dk_w, dv_w, st_c] + st_all,
        scratch=[
            pltpu.VMEM((tok, 128), F32),
            pltpu.VMEM((total, 128), F32),
            pltpu.VMEM((tok, 2 * hd), BF16),
        ],
        smem=(0, 1, 2, 3),
        flops=wide,
    )
    return (attn_out, query_grad, key_grad, value_grad)


def solution(mesh):
    rows = P("seq", "head")
    return jax.shard_map(
        on_device,
        mesh=mesh,
        in_specs=(rows, rows, rows, rows, P(("seq", "head"))),
        out_specs=(rows, rows, rows, rows),
        check_vma=False,
    )
```

```python
import functools
import math

import jax
import jax.numpy as jnp
from jax import lax
from jax.experimental import pallas as pl
from jax.experimental.pallas import tpu as pltpu
from jax.sharding import PartitionSpec as P

CLUS = 512
WINDOW = 512
F32 = jnp.float32
BF16 = jnp.bfloat16
NEG = -1e30
LANES = 128

NN = (((1,), (0,)), ((), ()))
NT = (((1,), (1,)), ((), ()))


def dot(left, right, dims=NN):
    return lax.dot_general(left, right, dims, preferred_element_type=F32)


def call(body, outs, inputs, scratch=(), smem=(), smem_outs=(), anywhere=(), us=0.0, aliases=None, vmem=8):
    def space(i, scalar):
        if i in scalar:
            return pltpu.SMEM
        return pl.ANY if i in anywhere else pltpu.VMEM

    moved = sum(x.size * x.dtype.itemsize for x in list(inputs) + list(outs))
    return pl.pallas_call(
        body,
        out_shape=outs,
        in_specs=[pl.BlockSpec(memory_space=space(i, smem)) for i in range(len(inputs))],
        out_specs=[
            pl.BlockSpec(memory_space=pltpu.SMEM if i in smem_outs else pltpu.VMEM) for i in range(len(outs))
        ],
        scratch_shapes=list(scratch),
        input_output_aliases=aliases or {},
        compiler_params=pltpu.CompilerParams(vmem_limit_bytes=vmem * 1024 * 1024),
        cost_estimate=pl.CostEstimate(flops=int(us * 1.15e9), bytes_accessed=moved, transcendentals=0),
    )(*inputs)


def shape(*dims, dtype=BF16):
    return jax.ShapeDtypeStruct(dims, dtype)


def to_row(column):
    n = column.shape[0]
    same = lax.broadcasted_iota(jnp.int32, (n, n), 0) == lax.broadcasted_iota(jnp.int32, (n, n), 1)
    return jnp.sum(jnp.where(same, column, 0.0), axis=0, keepdims=True)


def aligned(index, size):
    return pl.ds(pl.multiple_of(index * size, size), size)


def payloads(bits, hd, members_ref, q, k, v, g, *refs):
    kv_c, qg_c, kv_w, qg_w = refs[:4]
    pieces, (both, rim, spread, entries, sems) = refs[4 : 3 + bits], refs[3 + bits :]
    me = lax.axis_index("seq")
    width = 2 * hd
    copies = [pltpu.make_async_copy(members_ref, entries, sems.at[8])]
    for i, (source, target, lo, at) in enumerate(
        (
            (k, kv_c, hd, 0),
            (v, kv_c, hd, hd),
            (q, qg_c, hd, 0),
            (g, qg_c, hd, hd),
            (k, kv_w, 0, 0),
            (v, kv_w, 0, hd),
            (q, qg_w, 0, 0),
            (g, qg_w, 0, hd),
        )
    ):
        copies.append(
            pltpu.make_async_copy(source.at[:, lo : lo + hd], target.at[:, at : at + hd], sems.at[i])
        )
    for copy in copies:
        copy.start()
    copies[0].wait()
    spread[...] = jnp.broadcast_to(entries[...], spread.shape)
    for copy in copies[1:5]:
        copy.wait()

    def choose(bit, target, zero, one):
        low = ((me >> bit) & 1) == 0

        @pl.when(low)
        def _():
            target[:, 0:width] = zero[...]

        @pl.when(jnp.logical_not(low))
        def _():
            target[:, 0:width] = one[...]

    for bit in range(1, bits):
        choose(bit, pieces[bit - 1], kv_c, qg_c)
    choose(0, both, kv_c, qg_c)
    for copy in copies[5:]:
        copy.wait()
    choose(0, rim, qg_w, kv_w)
    both[:, width : 2 * width] = kv_w[...]
    both[:, 2 * width :] = qg_w[...]


def neighbour(parity, near_ref, block, far_ref, targets, at):
    tok, width = far_ref.shape
    hd = width // 2
    near = (lax.axis_index("seq") & 1) == parity

    @pl.when(near)
    def _():
        for i, target in enumerate(targets):
            lo = block * width + i * hd
            target[at : at + tok] = near_ref[:, lo : lo + hd]

    @pl.when(jnp.logical_not(near))
    def _():
        for i, target in enumerate(targets):
            target[at : at + tok] = far_ref[:, i * hd : (i + 1) * hd]


def window_rows(q, g, keys, values, allowed, scale):
    s = jnp.where(allowed, dot(q, keys, NT) * scale, NEG)
    dp = dot(g, values, NT)
    top = jnp.max(s, axis=1, keepdims=True)
    e = jnp.exp(s - top)
    total = jnp.sum(e, axis=1, keepdims=True)
    p = e * (1.0 / total)
    delta = jnp.sum(p * dp, axis=1, keepdims=True)
    return p, dp, to_row(top + jnp.log(total)), to_row(delta)


def window_queries(tok, hd, tile, kv_ref, qg_ref, near_ref, far_ref, out_ref, dq_ref, st_ref, kx, vx):
    scale = 1.0 / math.sqrt(hd)
    neighbour(1, near_ref, 1, far_ref, (kx, vx), 0)
    kx[tok:] = kv_ref[:, 0:hd]
    vx[tok:] = kv_ref[:, hd:]
    first = jnp.where(lax.axis_index("seq") == 0, tok, 0)
    span = tok + tile
    row = lax.broadcasted_iota(jnp.int32, (tile, span), 0)
    col = lax.broadcasted_iota(jnp.int32, (tile, span), 1)
    for lo in range(0, tok, tile):
        here = slice(lo, lo + tile)
        keys = kx[lo : lo + span]
        values = vx[lo : lo + span]
        allowed = (col > row) & (col <= row + tok) & (col + lo >= first)
        p, dp, top, delta = window_rows(
            qg_ref[here, 0:hd], qg_ref[here, hd:], keys, values, allowed, scale
        )
        st_ref[0:1, here] = top
        st_ref[1:2, here] = delta
        out_ref[here, 0:hd] = dot(p.astype(BF16), values).astype(BF16)
        delta = jnp.sum(p * dp, axis=1, keepdims=True)
        ds = (p * (dp - delta) * scale).astype(BF16)
        dq_ref[here, 0:hd] = dot(ds, keys).astype(BF16)


def window_keys(tok, hd, tile, kv_ref, qg_ref, near_ref, far_ref, far_keys, st_ref, dk_ref, dv_ref, kx, vx, qx, gx, stx):
    scale = 1.0 / math.sqrt(hd)
    neighbour(0, near_ref, 1, far_keys, (kx, vx), tok)
    neighbour(0, near_ref, 2, far_ref, (qx, gx), tok)
    kx[0:tok] = kv_ref[:, 0:hd]
    vx[0:tok] = kv_ref[:, hd:]
    qx[0:tok] = qg_ref[:, 0:hd]
    gx[0:tok] = qg_ref[:, hd:]
    stx[:, 0:tok] = st_ref[...]
    last = jnp.where(lax.axis_index("seq") == lax.axis_size("seq") - 1, tok, 2 * tok)
    span = tok + tile
    row = lax.broadcasted_iota(jnp.int32, (tile, span), 0)
    col = lax.broadcasted_iota(jnp.int32, (tile, span), 1)
    for lo in range(0, tok, tile):
        there = slice(tok + lo, tok + lo + tile)
        allowed = (col > row) & (col <= row + tok)
        _, _, top, delta = window_rows(
            qx[there], gx[there], kx[lo : lo + span], vx[lo : lo + span], allowed, scale
        )
        stx[0:1, there] = top
        stx[1:2, there] = delta
    for lo in range(0, tok, tile):
        here = slice(lo, lo + tile)
        queries = qx[lo : lo + span]
        grads = gx[lo : lo + span]
        allowed = (col >= row) & (col < row + tok) & (col + lo < last)
        s = dot(kx[here], queries, NT) * scale
        p = jnp.exp(jnp.where(allowed, s - stx[0:1, lo : lo + span], NEG))
        dv_ref[here] = dot(p.astype(BF16), grads).astype(BF16)
        dp = dot(vx[here], grads, NT)
        ds = (p * (dp - stx[1:2, lo : lo + span]) * scale).astype(BF16)
        dk_ref[here] = dot(ds, queries).astype(BF16)


def log2(n):
    return n.bit_length() - 1


def make_tables(cfg, lists_smem, src_tab, pos_tab, chunk_tab, count):
    shards, g, tok = cfg["shards"], cfg["g"], cfg["tok"]
    for s in range(shards):
        count[s] = 0

    def step(m, carry):
        s = lists_smem[m >> log2(cfg["per_row"]), (m & (cfg["per_row"] - 1)) * g] >> log2(tok)
        pos = count[s]
        count[s] = pos + 1
        src_tab[m] = s
        pos_tab[m] = pos
        chunk_tab[s * shards + pos] = m
        return carry

    lax.fori_loop(0, cfg["chunks"], step, 0, unroll=min(cfg["chunks"], 64))


def build_order(cfg, lists_ref, chunk_tab, s, order_ref):
    shards, g, tok, per = cfg["shards"], cfg["g"], cfg["tok"], cfg["per"]
    sub = lax.broadcasted_iota(jnp.int32, (g, per), 0)
    lane = lax.broadcasted_iota(jnp.int32, (g, per), 1)
    token = lax.broadcasted_iota(jnp.int32, (g, tok), 1)

    def step(k, carry):
        m = chunk_tab[s * shards + k]
        row = lists_ref[pl.ds(m >> log2(cfg["per_row"]), 1), :] - s * tok
        picked = jnp.where(lane == sub + (m & (cfg["per_row"] - 1)) * g, row, 0).astype(F32)
        column = jnp.sum(picked, axis=1, keepdims=True).astype(jnp.int32)
        order_ref[aligned(k, g), :] = jnp.where(column == token, 1.0, 0.0).astype(BF16)
        return carry

    lax.fori_loop(0, shards, step, 0, unroll=min(shards, 8))


def place(cfg, chunk_tab, s, rows_ref, to_ref):
    shards, g = cfg["shards"], cfg["g"]

    def step(k, carry):
        m = chunk_tab[s * shards + k]
        to_ref[aligned(m, g), :] = rows_ref[aligned(k, g), :]
        return carry

    lax.fori_loop(0, shards, step, 0, unroll=min(shards, 8))


def sort_blocks(cfg, lists_ref, chunk_tab, masks, arrived, rows_ref, orders, sorted_rows):
    for i, (mask, block) in enumerate(zip(masks, arrived)):
        s = lax.axis_index("seq") ^ mask
        order, rows = orders.at[i % 2], sorted_rows.at[i % 2]
        build_order(cfg, lists_ref, chunk_tab, s, order)
        rows[...] = dot(order[...], block[:, 0 : rows.shape[1]]).astype(BF16)
        place(cfg, chunk_tab, s, rows, rows_ref)


def sort_early(cfg, masks, *refs):
    (lists_smem, lists_ref, kv_in, qg_in), refs = refs[:4], refs[4:]
    arrived, refs = refs[: len(masks)], refs[len(masks) :]
    rows_ref, qg_ref, kv_ref, back_ref, src_tab, pos_tab, chunk_tab, count, orders, sorted_rows = refs
    me = lax.axis_index("seq")
    make_tables(cfg, lists_smem, src_tab, pos_tab, chunk_tab, count)
    build_order(cfg, lists_ref, chunk_tab, me, orders.at[0])
    own = orders[0]
    back_ref[...] = jnp.transpose(own)
    qg_ref[...] = dot(own, qg_in[...]).astype(BF16)
    kv_ref[...] = dot(own, kv_in[...]).astype(BF16)
    place(cfg, chunk_tab, me, kv_ref, rows_ref)
    sort_blocks(cfg, lists_ref, chunk_tab, masks, arrived, rows_ref, orders, sorted_rows)


def cluster_scores(cfg, masks, *refs):
    shards, g, hd = cfg["shards"], cfg["g"], cfg["hd"]
    (lists_ref, chunk_tab, qg_ref, rows_in), refs = refs[:4], refs[4:]
    arrived, refs = refs[: len(masks)], refs[len(masks) :]
    rows_ref, p_ref, ds_ref, st_ref, orders, sorted_rows = refs
    del rows_in
    scale = 1.0 / math.sqrt(hd)
    me = lax.axis_index("seq")
    sort_blocks(cfg, lists_ref, chunk_tab, masks, arrived, rows_ref, orders, sorted_rows)
    key_at = lax.broadcasted_iota(jnp.int32, (g, CLUS), 1)
    query_at = lax.broadcasted_iota(jnp.int32, (g, CLUS), 0)

    def step(k, carry):
        m = chunk_tab[me * shards + k]
        rank = (m & (shards - 1)) * g
        mine = aligned(k, g)
        whole = aligned(m >> log2(shards), CLUS)
        s = dot(qg_ref[mine, 0:hd], rows_ref[whole, 0:hd], NT) * scale
        dp = dot(qg_ref[mine, hd:], rows_ref[whole, hd:], NT)
        s = jnp.where(key_at <= query_at + rank, s, NEG)
        top = jnp.max(s, axis=1, keepdims=True)
        e = jnp.exp(s - top)
        total = jnp.sum(e, axis=1, keepdims=True)
        p = e * (1.0 / total)
        delta = jnp.sum(p * dp, axis=1, keepdims=True)
        p_ref[mine, :] = p.astype(BF16)
        ds_ref[mine, :] = (p * (dp - delta) * scale).astype(BF16)
        st_ref[pl.ds(k, 1), 0:g] = to_row(top + jnp.log(total))
        st_ref[pl.ds(shards + k, 1), 0:g] = to_row(delta)
        return carry

    lax.fori_loop(0, shards, step, 0, unroll=min(shards, 8))


def finish_queries(cfg, tile, *refs):
    shards, g, hd = cfg["shards"], cfg["g"], cfg["hd"]
    (chunk_tab, rows_ref, p_ref, ds_ref, back_ref), refs = refs[:5], refs[5:]
    kvw_ref, qgw_ref, near_ref, far_ref, out_ref, dq_ref, st_ref, outs, kx, vx = refs
    me = lax.axis_index("seq")

    def step(k, carry):
        m = chunk_tab[me * shards + k]
        mine = aligned(k, g)
        whole = aligned(m >> log2(shards), CLUS)
        outs[mine, 0:hd] = dot(p_ref[mine, :], rows_ref[whole, hd:]).astype(BF16)
        outs[mine, hd:] = dot(ds_ref[mine, :], rows_ref[whole, 0:hd]).astype(BF16)
        return carry

    lax.fori_loop(0, shards, step, 0, unroll=min(shards, 8))
    back = dot(back_ref[...], outs[...]).astype(BF16)
    out_ref[:, hd:] = back[:, 0:hd]
    dq_ref[:, hd:] = back[:, hd:]
    window_queries(cfg["tok"], hd, tile, kvw_ref, qgw_ref, near_ref, far_ref, out_ref, dq_ref, st_ref, kx, vx)


def cluster_keys(cfg, *refs):
    shards, g, hd = cfg["shards"], cfg["g"], cfg["hd"]
    (src_tab, pos_tab, chunk_tab, rows_in, qg_ref, kv_ref, back_ref, dkw_ref, dvw_ref, st_ref), refs = refs[:10], refs[10:]
    arrived, refs = refs[: shards - 1], refs[shards - 1 :]
    rows_ref, dk_ref, dv_ref, stats, outs = refs
    del rows_in
    scale = 1.0 / math.sqrt(hd)
    me = lax.axis_index("seq")
    place(cfg, chunk_tab, me, qg_ref, rows_ref)
    for mask in range(shards):
        st = st_ref if mask == 0 else arrived[mask - 1]
        stats[pl.ds(pl.multiple_of((me ^ mask) * 2 * shards, 2 * shards), 2 * shards), :] = st[...]
    query_at = lax.broadcasted_iota(jnp.int32, (g, CLUS), 1)
    key_at = lax.broadcasted_iota(jnp.int32, (g, CLUS), 0)

    def step(k, carry):
        m = chunk_tab[me * shards + k]
        first = m & ~(shards - 1)
        rank = (m & (shards - 1)) * g
        mine = aligned(k, g)
        whole = aligned(m >> log2(shards), CLUS)
        top, delta = [], []
        for j in range(shards):
            at = src_tab[first + j] * 2 * shards + pos_tab[first + j]
            top.append(stats[pl.ds(at, 1), 0:g])
            delta.append(stats[pl.ds(at + shards, 1), 0:g])
        queries = rows_ref[whole, 0:hd]
        grads = rows_ref[whole, hd:]
        s = dot(kv_ref[mine, 0:hd], queries, NT) * scale
        dp = dot(kv_ref[mine, hd:], grads, NT)
        allowed = query_at >= key_at + rank
        p = jnp.exp(jnp.where(allowed, s - jnp.concatenate(top, axis=1), NEG))
        ds = p * (dp - jnp.concatenate(delta, axis=1)) * scale
        outs[mine, 0:hd] = dot(ds.astype(BF16), queries).astype(BF16)
        outs[mine, hd:] = dot(p.astype(BF16), grads).astype(BF16)
        return carry

    lax.fori_loop(0, shards, step, 0, unroll=min(shards, 8))
    back = dot(back_ref[...], outs[...]).astype(BF16)
    dk_ref[:, 0:hd] = dkw_ref[...]
    dk_ref[:, hd:] = back[:, 0:hd]
    dv_ref[:, 0:hd] = dvw_ref[...]
    dv_ref[:, hd:] = back[:, hd:]


def partner(array, axis, mask):
    return lax.ppermute(array, axis, [(i, i ^ mask) for i in range(lax.axis_size(axis))])


def after(arrays, *earlier):
    return lax.optimization_barrier((arrays, earlier))[0]


def on_device(query_rows, key_rows, value_rows, out_grad, members):
    tok, width = query_rows.shape
    hd = width // 2
    shards = lax.axis_size("seq")
    heads = lax.axis_size("head")
    bits = log2(shards)
    me = lax.axis_index("seq")
    per = members.shape[0]
    total = per * shards * heads
    g = CLUS // shards
    cfg = dict(
        shards=shards, heads=heads, tok=tok, hd=hd, per=per, g=g, chunks=total // g, per_row=per // g
    )
    big = 2 if shards <= 8 else 4
    full = shape(tok, width)
    sides = [query_rows, key_rows, value_rows, out_grad]
    evens = list(range(2, shards, 2))

    kv_c, qg_c, kv_w, qg_w, *pieces, both, rim, spread = call(
        functools.partial(payloads, bits, hd),
        [full] * (bits + 3) + [shape(tok, 3 * width), full, shape(shards * heads, per, dtype=jnp.int32)],
        [pltpu.with_memory_space_constraint(x, pltpu.HBM) for x in [members.reshape(1, per)] + sides],
        scratch=[pltpu.VMEM((1, per), jnp.int32), pltpu.SemaphoreType.DMA((9,))],
        anywhere=(0, 1, 2, 3, 4),
        vmem=6 + bits,
    )
    got = {mask: partner(pieces[mask.bit_length() - 2], "seq", mask) for mask in evens}
    got[1] = partner(both, "seq", 1)
    lists = lax.all_to_all(after(spread, got[1]), ("seq", "head"), 0, 0, tiled=True)
    crossing = [(i, i + 1) for i in range(1, shards - 1, 2)] + [(shards - 1, 0)]
    crossing += [(b, a) for a, b in crossing]
    rim, rim_keys = after((rim, kv_w), lists)
    far = lax.ppermute(rim, "seq", crossing)
    far_keys = lax.ppermute(rim_keys, "seq", crossing)
    for mask in evens:
        got[mask + 1] = partner(after(got[mask], lists), "seq", 1)

    early = [1] + evens
    late = [mask + 1 for mask in evens]
    table = shape(total // g, dtype=jnp.int32)
    rows_shape = shape(total, 2 * hd)
    stat = shape(2 * shards, LANES, dtype=F32)
    orders = pltpu.VMEM((2, tok, tok), BF16)
    sorted_rows = pltpu.VMEM((2, tok, 2 * hd), BF16)

    rows, qg, kv, back, src, pos, chunk = call(
        functools.partial(sort_early, cfg, early),
        [rows_shape, full, full, shape(tok, tok), table, table, table],
        [lists, lists, kv_c, qg_c] + [got[mask] for mask in early],
        scratch=[pltpu.SMEM((shards,), jnp.int32), orders, sorted_rows],
        smem=(0,),
        smem_outs=(4, 5, 6),
        us=2.7,
        vmem=10 * big,
    )
    rows, p, ds, st_c = call(
        functools.partial(cluster_scores, cfg, late),
        [rows_shape, shape(tok, CLUS), shape(tok, CLUS), stat],
        [lists, chunk, qg, rows] + [got[mask] for mask in late],
        scratch=[orders, sorted_rows],
        smem=(1,),
        us=2.6,
        aliases={3: 0},
        vmem=6 * big,
    )
    tile = 256
    st = {mask: partner(st_c, "seq", mask) for mask in [1] + evens}
    attn_out, query_grad, st_w = call(
        functools.partial(finish_queries, cfg, tile),
        [full, full, shape(8, tok, dtype=F32)],
        [chunk, rows, p, ds, back, kv_w, qg_w, got[1], far],
        scratch=[pltpu.VMEM((tok, 2 * hd), BF16)] + [pltpu.VMEM((2 * tok, hd), BF16)] * 2,
        smem=(0,),
        us=3.7,
        vmem=5 * big,
    )
    for mask in evens:
        st[mask + 1] = partner(after(st[mask], st_w), "seq", 1)
    dk_w, dv_w = call(
        functools.partial(window_keys, tok, hd, tile),
        [shape(tok, hd)] * 2,
        [kv_w, qg_w, got[1], far, far_keys, st_w],
        scratch=[pltpu.VMEM((2 * tok, hd), BF16)] * 4 + [pltpu.VMEM((8, 2 * tok), F32)],
        us=2.1,
        vmem=10,
    )
    _, key_grad, value_grad = call(
        functools.partial(cluster_keys, cfg),
        [rows_shape, full, full],
        [src, pos, chunk, rows, qg, kv, back, dk_w, dv_w, st_c] + [st[mask] for mask in range(1, shards)],
        scratch=[pltpu.VMEM((2 * shards * shards, LANES), F32), pltpu.VMEM((tok, 2 * hd), BF16)],
        smem=(0, 1, 2),
        us=3.7,
        aliases={3: 0},
        vmem=4 * big,
    )
    return (attn_out, query_grad, key_grad, value_grad)


def solution(mesh):
    rows = P("seq", "head")
    return jax.shard_map(
        on_device,
        mesh=mesh,
        in_specs=(rows, rows, rows, rows, P(("seq", "head"))),
        out_specs=(rows, rows, rows, rows),
        check_vma=False,
    )
```

```python
import functools
import math

import jax
import jax.numpy as jnp
from jax import lax
from jax.experimental import pallas as pl
from jax.experimental.pallas import tpu as pltpu
from jax.sharding import PartitionSpec as P

CLUS = 512
WINDOW = 512
F32 = jnp.float32
BF16 = jnp.bfloat16
NEG = -1e30
LANES = 128

NN = (((1,), (0,)), ((), ()))
NT = (((1,), (1,)), ((), ()))


def dot(left, right, dims=NN):
    return lax.dot_general(left, right, dims, preferred_element_type=F32)


def call(body, outs, inputs, scratch=(), smem=(), hbm_outs=(), anywhere=(), us=0.0, aliases=None, vmem=8):
    def space(i, scalar):
        if i in scalar:
            return pltpu.SMEM
        return pl.ANY if i in anywhere else pltpu.VMEM

    moved = sum(x.size * x.dtype.itemsize for x in list(inputs) + list(outs))
    return pl.pallas_call(
        body,
        out_shape=outs,
        in_specs=[pl.BlockSpec(memory_space=space(i, smem)) for i in range(len(inputs))],
        out_specs=[
            pl.BlockSpec(memory_space=pl.ANY if i in hbm_outs else pltpu.VMEM) for i in range(len(outs))
        ],
        scratch_shapes=list(scratch),
        input_output_aliases=aliases or {},
        compiler_params=pltpu.CompilerParams(vmem_limit_bytes=vmem * 1024 * 1024),
        cost_estimate=pl.CostEstimate(flops=int(us * 1.15e9), bytes_accessed=moved, transcendentals=0),
    )(*inputs)


def shape(*dims, dtype=BF16):
    return jax.ShapeDtypeStruct(dims, dtype)


def to_row(column):
    n = column.shape[0]
    same = lax.broadcasted_iota(jnp.int32, (n, n), 0) == lax.broadcasted_iota(jnp.int32, (n, n), 1)
    return jnp.sum(jnp.where(same, column, 0.0), axis=0, keepdims=True)


def aligned(index, size):
    return pl.ds(pl.multiple_of(index * size, size), size)


def payloads(bits, hd, members_ref, q, k, v, g, *refs):
    kv_c, qg_c, kv_w, qg_w = refs[:4]
    pieces, (both, rim, spread, entries, sems) = refs[4 : 3 + bits], refs[3 + bits :]
    me = lax.axis_index("seq")
    width = 2 * hd
    copies = [pltpu.make_async_copy(members_ref, entries, sems.at[8])]
    for i, (source, target, lo, at) in enumerate(
        (
            (k, kv_c, hd, 0),
            (v, kv_c, hd, hd),
            (q, qg_c, hd, 0),
            (g, qg_c, hd, hd),
            (k, kv_w, 0, 0),
            (v, kv_w, 0, hd),
            (q, qg_w, 0, 0),
            (g, qg_w, 0, hd),
        )
    ):
        copies.append(
            pltpu.make_async_copy(source.at[:, lo : lo + hd], target.at[:, at : at + hd], sems.at[i])
        )
    for copy in copies:
        copy.start()
    copies[0].wait()
    spread[...] = jnp.broadcast_to(entries[...], spread.shape)
    for copy in copies[1:5]:
        copy.wait()

    def choose(bit, target, zero, one):
        low = ((me >> bit) & 1) == 0

        @pl.when(low)
        def _():
            target[:, 0:width] = zero[...]

        @pl.when(jnp.logical_not(low))
        def _():
            target[:, 0:width] = one[...]

    for bit in range(1, bits):
        choose(bit, pieces[bit - 1], kv_c, qg_c)
    choose(0, both, kv_c, qg_c)
    for copy in copies[5:]:
        copy.wait()
    choose(0, rim, qg_w, kv_w)
    both[:, width : 2 * width] = kv_w[...]
    both[:, 2 * width :] = qg_w[...]


def neighbour(parity, near_ref, block, far_ref, targets, at):
    tok, width = far_ref.shape
    hd = width // 2
    near = (lax.axis_index("seq") & 1) == parity

    @pl.when(near)
    def _():
        for i, target in enumerate(targets):
            lo = block * width + i * hd
            target[at : at + tok] = near_ref[:, lo : lo + hd]

    @pl.when(jnp.logical_not(near))
    def _():
        for i, target in enumerate(targets):
            target[at : at + tok] = far_ref[:, i * hd : (i + 1) * hd]


def window_rows(q, g, keys, values, allowed, scale):
    s = jnp.where(allowed, dot(q, keys, NT) * scale, NEG)
    dp = dot(g, values, NT)
    top = jnp.max(s, axis=1, keepdims=True)
    e = jnp.exp(s - top)
    total = jnp.sum(e, axis=1, keepdims=True)
    p = e * (1.0 / total)
    delta = jnp.sum(p * dp, axis=1, keepdims=True)
    return p, dp, to_row(top + jnp.log(total)), to_row(delta)


def window_queries(tok, hd, tile, kv_ref, qg_ref, near_ref, far_ref, done_ref, out_ref, dq_ref, st_ref, kx, vx):
    scale = 1.0 / math.sqrt(hd)
    neighbour(1, near_ref, 1, far_ref, (kx, vx), 0)
    out_ref[:, hd:] = done_ref[:, 0:hd]
    dq_ref[:, hd:] = done_ref[:, hd:]
    kx[tok:] = kv_ref[:, 0:hd]
    vx[tok:] = kv_ref[:, hd:]
    first = jnp.where(lax.axis_index("seq") == 0, tok, 0)
    span = tok + tile
    row = lax.broadcasted_iota(jnp.int32, (tile, span), 0)
    col = lax.broadcasted_iota(jnp.int32, (tile, span), 1)
    for lo in range(0, tok, tile):
        here = slice(lo, lo + tile)
        keys = kx[lo : lo + span]
        values = vx[lo : lo + span]
        allowed = (col > row) & (col <= row + tok) & (col + lo >= first)
        p, dp, top, delta = window_rows(
            qg_ref[here, 0:hd], qg_ref[here, hd:], keys, values, allowed, scale
        )
        st_ref[0:1, here] = top
        st_ref[1:2, here] = delta
        out_ref[here, 0:hd] = dot(p.astype(BF16), values).astype(BF16)
        delta = jnp.sum(p * dp, axis=1, keepdims=True)
        ds = (p * (dp - delta) * scale).astype(BF16)
        dq_ref[here, 0:hd] = dot(ds, keys).astype(BF16)


def window_keys(tok, hd, tile, *refs):
    kv_ref, qg_ref, near_ref, far_ref, st_ref, near_st, far_st, dk_ref, dv_ref, qx, gx, stx = refs
    scale = 1.0 / math.sqrt(hd)
    neighbour(0, near_ref, 2, far_ref, (qx, gx), tok)
    qx[0:tok] = qg_ref[:, 0:hd]
    gx[0:tok] = qg_ref[:, hd:]
    stx[:, 0:tok] = st_ref[...]
    even = (lax.axis_index("seq") & 1) == 0

    @pl.when(even)
    def _():
        stx[:, tok:] = near_st[...]

    @pl.when(jnp.logical_not(even))
    def _():
        stx[:, tok:] = far_st[...]

    last = jnp.where(lax.axis_index("seq") == lax.axis_size("seq") - 1, tok, 2 * tok)
    span = tok + tile
    row = lax.broadcasted_iota(jnp.int32, (tile, span), 0)
    col = lax.broadcasted_iota(jnp.int32, (tile, span), 1)
    for lo in range(0, tok, tile):
        here = slice(lo, lo + tile)
        queries = qx[lo : lo + span]
        grads = gx[lo : lo + span]
        allowed = (col >= row) & (col < row + tok) & (col + lo < last)
        s = dot(kv_ref[here, 0:hd], queries, NT) * scale
        p = jnp.exp(jnp.where(allowed, s - stx[0:1, lo : lo + span], NEG))
        dv_ref[here] = dot(p.astype(BF16), grads).astype(BF16)
        dp = dot(kv_ref[here, hd:], grads, NT)
        ds = (p * (dp - stx[1:2, lo : lo + span]) * scale).astype(BF16)
        dk_ref[here] = dot(ds, queries).astype(BF16)


def log2(n):
    return n.bit_length() - 1


def make_tables(cfg, lists_smem, tab, count):
    shards, g, tok, chunks = cfg["shards"], cfg["g"], cfg["tok"], cfg["chunks"]
    for s in range(shards):
        count[s] = 0

    def step(m, carry):
        s = lists_smem[m >> log2(cfg["per_row"]), (m & (cfg["per_row"] - 1)) * g] >> log2(tok)
        pos = count[s]
        count[s] = pos + 1
        tab[m] = s
        tab[chunks + m] = pos
        tab[2 * chunks + s * shards + pos] = m
        return carry

    lax.fori_loop(0, chunks, step, 0, unroll=min(chunks, 64))


def chunk_of(cfg, tab, s, k):
    return tab[2 * cfg["chunks"] + s * cfg["shards"] + k]


def make_columns(cfg, lists_ref, columns):
    tok, per = cfg["tok"], cfg["per"]
    same = lax.broadcasted_iota(jnp.int32, (per, per), 0) == lax.broadcasted_iota(jnp.int32, (per, per), 1)
    rows = lists_ref.shape[0]

    def step(r, carry):
        row = (lists_ref[pl.ds(r, 1), :] & (tok - 1)).astype(F32)
        columns[aligned(r, per), 0:1] = jnp.sum(jnp.where(same, row, 0.0), axis=1, keepdims=True)
        return carry

    lax.fori_loop(0, rows, step, 0, unroll=min(rows, 32))


def build_order(cfg, columns, tab, s, order_ref):
    shards, g, tok = cfg["shards"], cfg["g"], cfg["tok"]
    token = lax.broadcasted_iota(jnp.int32, (g, tok), 1).astype(F32)

    def step(k, carry):
        column = columns[aligned(chunk_of(cfg, tab, s, k), g), 0:1]
        order_ref[aligned(k, g), :] = jnp.where(column == token, 1.0, 0.0).astype(BF16)
        return carry

    lax.fori_loop(0, shards, step, 0, unroll=min(shards, 8))


def place(cfg, tab, s, rows_ref, to_ref):
    shards, g = cfg["shards"], cfg["g"]

    def step(k, carry):
        m = chunk_of(cfg, tab, s, k)
        to_ref[aligned(m, g), :] = rows_ref[aligned(k, g), :]
        return carry

    lax.fori_loop(0, shards, step, 0, unroll=min(shards, 8))


def sort_blocks(cfg, columns, tab, masks, arrived, rows_ref, orders, sorted_rows):
    for i, (mask, block) in enumerate(zip(masks, arrived)):
        s = lax.axis_index("seq") ^ mask
        order, rows = orders.at[i % 2], sorted_rows.at[i % 2]
        build_order(cfg, columns, tab, s, order)
        rows[...] = dot(order[...], block[:, 0 : rows.shape[1]]).astype(BF16)
        place(cfg, tab, s, rows, rows_ref)


def sort_and_score(cfg, *refs):
    shards, g, hd = cfg["shards"], cfg["g"], cfg["hd"]
    (lists_ref, kv_in, qg_in), refs = refs[:3], refs[3:]
    arrived, refs = refs[: shards - 1], refs[shards - 1 :]
    rows_ref, qg_ref, kv_ref, back_ref, p_ref, ds_ref, st_ref, tab_out = refs[:8]
    lists_smem, tab, count, sems, columns, orders, sorted_rows = refs[8:]
    scale = 1.0 / math.sqrt(hd)
    me = lax.axis_index("seq")
    load = pltpu.make_async_copy(lists_ref, lists_smem, sems.at[0])
    load.start()
    make_columns(cfg, lists_ref, columns)
    load.wait()
    make_tables(cfg, lists_smem, tab, count)
    keep = pltpu.make_async_copy(tab, tab_out, sems.at[1])
    keep.start()
    build_order(cfg, columns, tab, me, orders.at[0])
    own = orders[0]
    back_ref[...] = jnp.transpose(own)
    qg_ref[...] = dot(own, qg_in[...]).astype(BF16)
    kv_ref[...] = dot(own, kv_in[...]).astype(BF16)
    place(cfg, tab, me, kv_ref, rows_ref)
    sort_blocks(cfg, columns, tab, range(1, shards), arrived, rows_ref, orders, sorted_rows)
    key_at = lax.broadcasted_iota(jnp.int32, (g, CLUS), 1)
    query_at = lax.broadcasted_iota(jnp.int32, (g, CLUS), 0)

    def step(k, carry):
        m = chunk_of(cfg, tab, me, k)
        rank = (m & (shards - 1)) * g
        mine = aligned(k, g)
        whole = aligned(m >> log2(shards), CLUS)
        s = dot(qg_ref[mine, 0:hd], rows_ref[whole, 0:hd], NT) * scale
        dp = dot(qg_ref[mine, hd:], rows_ref[whole, hd:], NT)
        s = jnp.where(key_at <= query_at + rank, s, NEG)
        top = jnp.max(s, axis=1, keepdims=True)
        e = jnp.exp(s - top)
        total = jnp.sum(e, axis=1, keepdims=True)
        p = e * (1.0 / total)
        delta = jnp.sum(p * dp, axis=1, keepdims=True)
        p_ref[mine, :] = p.astype(BF16)
        ds_ref[mine, :] = (p * (dp - delta) * scale).astype(BF16)
        st_ref[pl.ds(k, 1), 0:g] = to_row(top + jnp.log(total))
        st_ref[pl.ds(shards + k, 1), 0:g] = to_row(delta)
        return carry

    lax.fori_loop(0, shards, step, 0, unroll=min(shards, 8))
    keep.wait()


def join(own_ref, other_ref, out_ref):
    rows = own_ref.shape[0]
    out_ref[0:rows] = own_ref[...]
    out_ref[rows:] = other_ref[...]


def cluster_queries(cfg, *refs):
    shards, g, hd = cfg["shards"], cfg["g"], cfg["hd"]
    tab, rows_ref, p_ref, ds_ref, back_ref, done_ref, outs = refs
    me = lax.axis_index("seq")

    def step(k, carry):
        m = chunk_of(cfg, tab, me, k)
        mine = aligned(k, g)
        whole = aligned(m >> log2(shards), CLUS)
        outs[mine, 0:hd] = dot(p_ref[mine, :], rows_ref[whole, hd:]).astype(BF16)
        outs[mine, hd:] = dot(ds_ref[mine, :], rows_ref[whole, 0:hd]).astype(BF16)
        return carry

    lax.fori_loop(0, shards, step, 0, unroll=min(shards, 8))
    done_ref[...] = dot(back_ref[...], outs[...]).astype(BF16)


def key_scores(cfg, *refs):
    shards, g, hd = cfg["shards"], cfg["g"], cfg["hd"]
    tab, rows_in, qg_ref, kv_ref, rows_ref, s_ref, dp_ref = refs
    del rows_in
    scale = 1.0 / math.sqrt(hd)
    me = lax.axis_index("seq")
    place(cfg, tab, me, qg_ref, rows_ref)

    def step(k, carry):
        mine = aligned(k, g)
        whole = aligned(chunk_of(cfg, tab, me, k) >> log2(shards), CLUS)
        s_ref[mine, :] = dot(kv_ref[mine, 0:hd], rows_ref[whole, 0:hd], NT) * scale
        dp_ref[mine, :] = dot(kv_ref[mine, hd:], rows_ref[whole, hd:], NT)
        return carry

    lax.fori_loop(0, shards, step, 0, unroll=min(shards, 8))


def cluster_keys(cfg, *refs):
    shards, g, hd = cfg["shards"], cfg["g"], cfg["hd"]
    tab, rows_ref, back_ref, s_ref, dp_ref, dkw_ref, dvw_ref, near_ref, far_ref, out_in, dq_in = refs[:11]
    out_ref, dq_ref, dk_ref, dv_ref, stats, outs, sems = refs[11:]
    scale = 1.0 / math.sqrt(hd)
    me = lax.axis_index("seq")
    copies = [
        pltpu.make_async_copy(out_in, out_ref, sems.at[0]),
        pltpu.make_async_copy(dq_in, dq_ref, sems.at[1]),
    ]
    for copy in copies:
        copy.start()
    join(near_ref, far_ref, stats)
    query_at = lax.broadcasted_iota(jnp.int32, (g, CLUS), 1)
    key_at = lax.broadcasted_iota(jnp.int32, (g, CLUS), 0)

    def step(k, carry):
        m = chunk_of(cfg, tab, me, k)
        first = m & ~(shards - 1)
        rank = (m & (shards - 1)) * g
        mine = aligned(k, g)
        whole = aligned(m >> log2(shards), CLUS)
        top, delta = [], []
        for j in range(shards):
            at = (tab[first + j] ^ me) * 2 * shards + tab[cfg["chunks"] + first + j]
            top.append(stats[pl.ds(at, 1), 0:g])
            delta.append(stats[pl.ds(at + shards, 1), 0:g])
        allowed = query_at >= key_at + rank
        p = jnp.exp(jnp.where(allowed, s_ref[mine, :] - jnp.concatenate(top, axis=1), NEG))
        ds = p * (dp_ref[mine, :] - jnp.concatenate(delta, axis=1)) * scale
        outs[mine, 0:hd] = dot(ds.astype(BF16), rows_ref[whole, 0:hd]).astype(BF16)
        outs[mine, hd:] = dot(p.astype(BF16), rows_ref[whole, hd:]).astype(BF16)
        return carry

    lax.fori_loop(0, shards, step, 0, unroll=min(shards, 8))
    back = dot(back_ref[...], outs[...]).astype(BF16)
    dk_ref[:, 0:hd] = dkw_ref[...]
    dk_ref[:, hd:] = back[:, 0:hd]
    dv_ref[:, 0:hd] = dvw_ref[...]
    dv_ref[:, hd:] = back[:, hd:]
    for copy in copies:
        copy.wait()


def partner(array, axis, mask):
    return lax.ppermute(array, axis, [(i, i ^ mask) for i in range(lax.axis_size(axis))])


def after(arrays, *earlier):
    return lax.optimization_barrier((arrays, earlier))[0]


def on_device(query_rows, key_rows, value_rows, out_grad, members):
    tok, width = query_rows.shape
    assert tok == WINDOW
    hd = width // 2
    shards = lax.axis_size("seq")
    heads = lax.axis_size("head")
    bits = log2(shards)
    me = lax.axis_index("seq")
    per = members.shape[0]
    total = per * shards * heads
    g = CLUS // shards
    cfg = dict(
        shards=shards, heads=heads, tok=tok, hd=hd, per=per, g=g, chunks=total // g, per_row=per // g
    )
    big = 2 if shards <= 8 else 4
    full = shape(tok, width)
    sides = [query_rows, key_rows, value_rows, out_grad]
    evens = list(range(2, shards, 2))

    kv_c, qg_c, kv_w, qg_w, *pieces, both, rim, spread = call(
        functools.partial(payloads, bits, hd),
        [full] * (bits + 3) + [shape(tok, 3 * width), full, shape(shards * heads, per, dtype=jnp.int32)],
        [pltpu.with_memory_space_constraint(x, pltpu.HBM) for x in [members.reshape(1, per)] + sides],
        scratch=[pltpu.VMEM((1, per), jnp.int32), pltpu.SemaphoreType.DMA((9,))],
        anywhere=(0, 1, 2, 3, 4),
        vmem=6 + bits,
    )
    got = {mask: partner(pieces[mask.bit_length() - 2], "seq", mask) for mask in evens}
    got[1] = partner(both, "seq", 1)
    lists = lax.all_to_all(after(spread, got[1]), ("seq", "head"), 0, 0, tiled=True)
    crossing = [(i, i + 1) for i in range(1, shards - 1, 2)] + [(shards - 1, 0)]
    crossing += [(b, a) for a, b in crossing]
    far = lax.ppermute(after(rim, lists), "seq", crossing)
    for mask in evens:
        got[mask + 1] = partner(after(got[mask], lists), "seq", 1)

    table = 3 * (total // g)
    rows_shape = shape(total, 2 * hd)
    stat = shape(2 * shards, LANES, dtype=F32)
    rows, qg, kv, back, p, ds, st_c, tab = call(
        functools.partial(sort_and_score, cfg),
        [rows_shape, full, full, shape(tok, tok), shape(tok, CLUS), shape(tok, CLUS), stat, shape(table, dtype=jnp.int32)],
        [lists, kv_c, qg_c] + [got[mask] for mask in range(1, shards)],
        scratch=[
            pltpu.SMEM((shards * heads, per), jnp.int32),
            pltpu.SMEM((table,), jnp.int32),
            pltpu.SMEM((shards,), jnp.int32),
            pltpu.SemaphoreType.DMA((2,)),
            pltpu.VMEM((total, LANES), F32),
            pltpu.VMEM((2, tok, tok), BF16),
            pltpu.VMEM((2, tok, 2 * hd), BF16),
        ],
        us=5.0,
        vmem=12 * big,
    )
    tile = 256
    def gather_step(held, bit, *earlier):
        return held, partner(after(held, *earlier), "seq", 1 << bit)

    def joined(held, other):
        rows_of = held.shape[0]
        return call(join, [shape(2 * rows_of, LANES, dtype=F32)], [held, other], vmem=2)[0]

    held, other = gather_step(st_c, 0)
    (done,) = call(
        functools.partial(cluster_queries, cfg),
        [full],
        [tab, rows, p, ds, back],
        scratch=[pltpu.VMEM((tok, 2 * hd), BF16)],
        smem=(0,),
        us=1.5,
        vmem=4 * big,
    )
    for bit in range(1, bits - 1):
        held, other = gather_step(joined(held, after(other, done)), bit)
    out_all, dq_all, st_w = call(
        functools.partial(window_queries, tok, hd, tile),
        [full, full, shape(8, tok, dtype=F32)],
        [kv_w, qg_w, got[1], far, after(done, held)],
        scratch=[pltpu.VMEM((2 * tok, hd), BF16)] * 2,
        us=1.7,
        vmem=8,
    )
    near_st = partner(st_w, "seq", 1)
    far_st = lax.ppermute(st_w, "seq", crossing)
    held, other = gather_step(joined(held, after(other, st_w)), bits - 1)
    rows, s, dp = call(
        functools.partial(key_scores, cfg),
        [rows_shape, shape(tok, CLUS, dtype=F32), shape(tok, CLUS, dtype=F32)],
        [tab, rows, qg, after(kv, held)],
        smem=(0,),
        us=0.4,
        aliases={1: 0},
        vmem=4 * big,
    )
    dk_w, dv_w = call(
        functools.partial(window_keys, tok, hd, tile),
        [shape(tok, hd)] * 2,
        [kv_w, qg_w, got[1], far, after(st_w, s), near_st, far_st],
        scratch=[pltpu.VMEM((2 * tok, hd), BF16)] * 2 + [pltpu.VMEM((8, 2 * tok), F32)],
        us=0.2,
        vmem=8,
    )
    return call(
        functools.partial(cluster_keys, cfg),
        [full] * 4,
        [tab, rows, back, s, dp, dk_w, dv_w, held, other, out_all, dq_all],
        scratch=[
            pltpu.VMEM((2 * shards * shards, LANES), F32),
            pltpu.VMEM((tok, 2 * hd), BF16),
            pltpu.SemaphoreType.DMA((2,)),
        ],
        smem=(0,),
        hbm_outs=(0, 1),
        us=2.6,
        vmem=4 * big,
    )


def solution(mesh):
    rows = P("seq", "head")
    return jax.shard_map(
        on_device,
        mesh=mesh,
        in_specs=(rows, rows, rows, rows, P(("seq", "head"))),
        out_specs=(rows, rows, rows, rows),
        check_vma=False,
    )
```

```python
import functools
import math

import jax
import jax.numpy as jnp
from jax import lax
from jax.experimental import pallas as pl
from jax.experimental.pallas import tpu as pltpu
from jax.sharding import PartitionSpec as P

CLUS = 512
WINDOW = 512
F32 = jnp.float32
BF16 = jnp.bfloat16
NEG = -1e30
LANES = 128

NN = (((1,), (0,)), ((), ()))
NT = (((1,), (1,)), ((), ()))


def dot(left, right, dims=NN):
    return lax.dot_general(left, right, dims, preferred_element_type=F32)


def call(body, outs, inputs, scratch=(), smem=(), hbm_outs=(), anywhere=(), us=0.0, aliases=None, vmem=8):
    def space(i, scalar):
        if i in scalar:
            return pltpu.SMEM
        return pl.ANY if i in anywhere else pltpu.VMEM

    moved = sum(x.size * x.dtype.itemsize for x in list(inputs) + list(outs))
    return pl.pallas_call(
        body,
        out_shape=outs,
        in_specs=[pl.BlockSpec(memory_space=space(i, smem)) for i in range(len(inputs))],
        out_specs=[
            pl.BlockSpec(memory_space=pl.ANY if i in hbm_outs else pltpu.VMEM) for i in range(len(outs))
        ],
        scratch_shapes=list(scratch),
        input_output_aliases=aliases or {},
        compiler_params=pltpu.CompilerParams(vmem_limit_bytes=vmem * 1024 * 1024),
        cost_estimate=pl.CostEstimate(flops=int(us * 1.15e9), bytes_accessed=moved, transcendentals=0),
    )(*inputs)


def shape(*dims, dtype=BF16):
    return jax.ShapeDtypeStruct(dims, dtype)


def to_row(column):
    n = column.shape[0]
    same = lax.broadcasted_iota(jnp.int32, (n, n), 0) == lax.broadcasted_iota(jnp.int32, (n, n), 1)
    return jnp.sum(jnp.where(same, column, 0.0), axis=0, keepdims=True)


def aligned(index, size):
    return pl.ds(pl.multiple_of(index * size, size), size)


def payloads(bits, hd, members_ref, q, k, v, g, *refs):
    kv_c, qg_c, kv_w, qg_w = refs[:4]
    pieces, (both, rim, spread, entries, repeated, sems) = refs[4 : 3 + bits], refs[3 + bits :]
    me = lax.axis_index("seq")
    width = 2 * hd
    copies = [pltpu.make_async_copy(members_ref, entries, sems.at[8])]
    for i, (source, target, lo, at) in enumerate(
        (
            (k, kv_c, hd, 0),
            (v, kv_c, hd, hd),
            (q, qg_c, hd, 0),
            (g, qg_c, hd, hd),
            (k, kv_w, 0, 0),
            (v, kv_w, 0, hd),
            (q, qg_w, 0, 0),
            (g, qg_w, 0, hd),
        )
    ):
        copies.append(
            pltpu.make_async_copy(source.at[:, lo : lo + hd], target.at[:, at : at + hd], sems.at[i])
        )
    for copy in copies:
        copy.start()
    copies[0].wait()
    repeated[...] = jnp.broadcast_to(entries[...], repeated.shape)
    copies.append(pltpu.make_async_copy(repeated, spread, sems.at[9]))
    copies[-1].start()
    for copy in copies[1:5]:
        copy.wait()

    def choose(bit, target, zero, one):
        low = ((me >> bit) & 1) == 0

        @pl.when(low)
        def _():
            target[:, 0:width] = zero[...]

        @pl.when(jnp.logical_not(low))
        def _():
            target[:, 0:width] = one[...]

    for bit in range(1, bits):
        choose(bit, pieces[bit - 1], kv_c, qg_c)
    choose(0, both, kv_c, qg_c)
    for copy in copies[5:]:
        copy.wait()
    choose(0, rim, qg_w, kv_w)
    both[:, width : 2 * width] = kv_w[...]
    both[:, 2 * width :] = qg_w[...]


def neighbour(parity, near_ref, block, far_ref, targets, at):
    tok, width = far_ref.shape
    hd = width // 2
    near = (lax.axis_index("seq") & 1) == parity

    @pl.when(near)
    def _():
        for i, target in enumerate(targets):
            lo = block * width + i * hd
            target[at : at + tok] = near_ref[:, lo : lo + hd]

    @pl.when(jnp.logical_not(near))
    def _():
        for i, target in enumerate(targets):
            target[at : at + tok] = far_ref[:, i * hd : (i + 1) * hd]


def window_rows(q, g, keys, values, allowed, scale):
    s = jnp.where(allowed, dot(q, keys, NT) * scale, NEG)
    dp = dot(g, values, NT)
    top = jnp.max(s, axis=1, keepdims=True)
    e = jnp.exp(s - top)
    total = jnp.sum(e, axis=1, keepdims=True)
    p = e * (1.0 / total)
    delta = jnp.sum(p * dp, axis=1, keepdims=True)
    return p, dp, to_row(top + jnp.log(total)), to_row(delta)


def window_scores(tok, hd, tile, *refs):
    kv_ref, qg_ref, near_ref, far_ref, p_ref, ds_ref, st_ref, kx, vx = refs
    scale = 1.0 / math.sqrt(hd)
    neighbour(1, near_ref, 1, far_ref, (kx, vx), 0)
    kx[tok:] = kv_ref[:, 0:hd]
    vx[tok:] = kv_ref[:, hd:]
    first = jnp.where(lax.axis_index("seq") == 0, tok, 0)
    span = tok + tile
    row = lax.broadcasted_iota(jnp.int32, (tile, span), 0)
    col = lax.broadcasted_iota(jnp.int32, (tile, span), 1)
    for lo in range(0, tok, tile):
        here = slice(lo, lo + tile)
        allowed = (col > row) & (col <= row + tok) & (col + lo >= first)
        s = jnp.where(allowed, dot(qg_ref[here, 0:hd], kx[lo : lo + span], NT) * scale, NEG)
        dp = dot(qg_ref[here, hd:], vx[lo : lo + span], NT)
        top = jnp.max(s, axis=1, keepdims=True)
        e = jnp.exp(s - top)
        total = jnp.sum(e, axis=1, keepdims=True)
        p = e * (1.0 / total)
        delta = jnp.sum(p * dp, axis=1, keepdims=True)
        p_ref[here, :] = p.astype(BF16)
        ds_ref[here, :] = (p * (dp - delta) * scale).astype(BF16)
        st_ref[0:1, here] = to_row(top + jnp.log(total))
        st_ref[1:2, here] = to_row(delta)


def query_outputs(tok, hd, tile, p_ref, ds_ref, kx, vx, back_ref, outs_ref, out_ref, dq_ref):
    span = tok + tile
    for lo in range(0, tok, tile):
        here = slice(lo, lo + tile)
        out_ref[here, 0:hd] = dot(p_ref[here, :], vx[lo : lo + span]).astype(BF16)
        dq_ref[here, 0:hd] = dot(ds_ref[here, :], kx[lo : lo + span]).astype(BF16)
    back = dot(back_ref[...], outs_ref[...]).astype(BF16)
    out_ref[:, hd:] = back[:, 0:hd]
    dq_ref[:, hd:] = back[:, hd:]


def window_keys(tok, hd, tile, *refs):
    kv_ref, qg_ref, near_ref, far_ref, st_ref, near_st, far_st, dk_ref, dv_ref, qx, gx, stx = refs
    scale = 1.0 / math.sqrt(hd)
    neighbour(0, near_ref, 2, far_ref, (qx, gx), tok)
    qx[0:tok] = qg_ref[:, 0:hd]
    gx[0:tok] = qg_ref[:, hd:]
    stx[:, 0:tok] = st_ref[...]
    even = (lax.axis_index("seq") & 1) == 0

    @pl.when(even)
    def _():
        stx[:, tok:] = near_st[...]

    @pl.when(jnp.logical_not(even))
    def _():
        stx[:, tok:] = far_st[...]

    last = jnp.where(lax.axis_index("seq") == lax.axis_size("seq") - 1, tok, 2 * tok)
    span = tok + tile
    row = lax.broadcasted_iota(jnp.int32, (tile, span), 0)
    col = lax.broadcasted_iota(jnp.int32, (tile, span), 1)
    for lo in range(0, tok, tile):
        here = slice(lo, lo + tile)
        queries = qx[lo : lo + span]
        grads = gx[lo : lo + span]
        allowed = (col >= row) & (col < row + tok) & (col + lo < last)
        s = dot(kv_ref[here, 0:hd], queries, NT) * scale
        p = jnp.exp(jnp.where(allowed, s - stx[0:1, lo : lo + span], NEG))
        dv_ref[here, 0:hd] = dot(p.astype(BF16), grads).astype(BF16)
        dp = dot(kv_ref[here, hd:], grads, NT)
        ds = (p * (dp - stx[1:2, lo : lo + span]) * scale).astype(BF16)
        dk_ref[here, 0:hd] = dot(ds, queries).astype(BF16)


def log2(n):
    return n.bit_length() - 1


def make_tables(cfg, lists_smem, tab, count):
    shards, g, tok, chunks = cfg["shards"], cfg["g"], cfg["tok"], cfg["chunks"]
    for s in range(shards):
        count[s] = 0

    def step(m, carry):
        s = lists_smem[m >> log2(cfg["per_row"]), (m & (cfg["per_row"] - 1)) * g] >> log2(tok)
        pos = count[s]
        count[s] = pos + 1
        tab[m] = s
        tab[chunks + m] = pos
        tab[2 * chunks + s * shards + pos] = m
        return carry

    lax.fori_loop(0, chunks, step, 0, unroll=min(chunks, 64))


def chunk_of(cfg, tab, s, k):
    return tab[2 * cfg["chunks"] + s * cfg["shards"] + k]


def make_columns(cfg, lists_ref, columns):
    tok, per = cfg["tok"], cfg["per"]
    same = lax.broadcasted_iota(jnp.int32, (per, per), 0) == lax.broadcasted_iota(jnp.int32, (per, per), 1)
    rows = lists_ref.shape[0]

    def step(r, carry):
        row = (lists_ref[pl.ds(r, 1), :] & (tok - 1)).astype(F32)
        columns[aligned(r, per), 0:1] = jnp.sum(jnp.where(same, row, 0.0), axis=1, keepdims=True)
        return carry

    lax.fori_loop(0, rows, step, 0, unroll=min(rows, 32))


def build_order(cfg, columns, tab, s, order_ref):
    shards, g, tok = cfg["shards"], cfg["g"], cfg["tok"]
    token = lax.broadcasted_iota(jnp.int32, (g, tok), 1).astype(F32)

    def step(k, carry):
        column = columns[aligned(chunk_of(cfg, tab, s, k), g), 0:1]
        order_ref[aligned(k, g), :] = jnp.where(column == token, 1.0, 0.0).astype(BF16)
        return carry

    lax.fori_loop(0, shards, step, 0, unroll=min(shards, 8))


def place(cfg, tab, s, rows_ref, to_ref):
    shards, g = cfg["shards"], cfg["g"]

    def step(k, carry):
        m = chunk_of(cfg, tab, s, k)
        to_ref[aligned(m, g), :] = rows_ref[aligned(k, g), :]
        return carry

    lax.fori_loop(0, shards, step, 0, unroll=min(shards, 8))


def sort_blocks(cfg, columns, tab, masks, arrived, rows_ref, orders, sorted_rows):
    for i, (mask, block) in enumerate(zip(masks, arrived)):
        s = lax.axis_index("seq") ^ mask
        order, rows = orders.at[i % 2], sorted_rows.at[i % 2]
        build_order(cfg, columns, tab, s, order)
        rows[...] = dot(order[...], block[:, 0 : rows.shape[1]]).astype(BF16)
        place(cfg, tab, s, rows, rows_ref)


def sort_and_score(cfg, *refs):
    shards, g, hd = cfg["shards"], cfg["g"], cfg["hd"]
    (lists_ref, kv_in, qg_in), refs = refs[:3], refs[3:]
    arrived, refs = refs[: shards - 1], refs[shards - 1 :]
    rows_ref, qg_ref, kv_ref, back_ref, p_ref, ds_ref, st_ref, tab_out = refs[:8]
    lists_smem, tab, count, sems, columns, orders, sorted_rows = refs[8:]
    scale = 1.0 / math.sqrt(hd)
    me = lax.axis_index("seq")
    load = pltpu.make_async_copy(lists_ref, lists_smem, sems.at[0])
    load.start()
    make_columns(cfg, lists_ref, columns)
    load.wait()
    make_tables(cfg, lists_smem, tab, count)
    keep = pltpu.make_async_copy(tab, tab_out, sems.at[1])
    keep.start()
    build_order(cfg, columns, tab, me, orders.at[0])
    own = orders[0]
    back_ref[...] = jnp.transpose(own)
    qg_ref[...] = dot(own, qg_in[...]).astype(BF16)
    kv_ref[...] = dot(own, kv_in[...]).astype(BF16)
    place(cfg, tab, me, kv_ref, rows_ref)
    sort_blocks(cfg, columns, tab, range(1, shards), arrived, rows_ref, orders, sorted_rows)
    key_at = lax.broadcasted_iota(jnp.int32, (g, CLUS), 1)
    query_at = lax.broadcasted_iota(jnp.int32, (g, CLUS), 0)

    def step(k, carry):
        m = chunk_of(cfg, tab, me, k)
        rank = (m & (shards - 1)) * g
        mine = aligned(k, g)
        whole = aligned(m >> log2(shards), CLUS)
        s = dot(qg_ref[mine, 0:hd], rows_ref[whole, 0:hd], NT) * scale
        dp = dot(qg_ref[mine, hd:], rows_ref[whole, hd:], NT)
        s = jnp.where(key_at <= query_at + rank, s, NEG)
        top = jnp.max(s, axis=1, keepdims=True)
        e = jnp.exp(s - top)
        total = jnp.sum(e, axis=1, keepdims=True)
        p = e * (1.0 / total)
        delta = jnp.sum(p * dp, axis=1, keepdims=True)
        p_ref[mine, :] = p.astype(BF16)
        ds_ref[mine, :] = (p * (dp - delta) * scale).astype(BF16)
        st_ref[pl.ds(k, 1), 0:g] = to_row(top + jnp.log(total))
        st_ref[pl.ds(shards + k, 1), 0:g] = to_row(delta)
        return carry

    lax.fori_loop(0, shards, step, 0, unroll=min(shards, 8))
    keep.wait()


def join(own_ref, other_ref, out_ref):
    rows = own_ref.shape[0]
    out_ref[0:rows] = own_ref[...]
    out_ref[rows:] = other_ref[...]


def finish_queries(cfg, *refs):
    shards, g, hd = cfg["shards"], cfg["g"], cfg["hd"]
    tab, rows_in, p_ref, ds_ref, qg_ref, kv_ref, rows_ref, outs, s_ref, dp_ref = refs
    del rows_in
    scale = 1.0 / math.sqrt(hd)
    me = lax.axis_index("seq")

    def query_step(k, carry):
        mine = aligned(k, g)
        whole = aligned(chunk_of(cfg, tab, me, k) >> log2(shards), CLUS)
        outs[mine, 0:hd] = dot(p_ref[mine, :], rows_ref[whole, hd:]).astype(BF16)
        outs[mine, hd:] = dot(ds_ref[mine, :], rows_ref[whole, 0:hd]).astype(BF16)
        return carry

    lax.fori_loop(0, shards, query_step, 0, unroll=min(shards, 8))
    place(cfg, tab, me, qg_ref, rows_ref)

    def key_step(k, carry):
        mine = aligned(k, g)
        whole = aligned(chunk_of(cfg, tab, me, k) >> log2(shards), CLUS)
        s_ref[mine, :] = dot(kv_ref[mine, 0:hd], rows_ref[whole, 0:hd], NT) * scale
        dp_ref[mine, :] = dot(kv_ref[mine, hd:], rows_ref[whole, hd:], NT)
        return carry

    lax.fori_loop(0, shards, key_step, 0, unroll=min(shards, 8))


def key_outputs(cfg, *refs):
    shards, g, hd = cfg["shards"], cfg["g"], cfg["hd"]
    tab, rows_ref, back_ref, s_ref, dp_ref, near_ref, far_ref, out_in, dq_in, dkw_ref, dvw_ref = refs[:11]
    out_ref, dq_ref, dk_ref, dv_ref, stats, outs, sems = refs[11:]
    scale = 1.0 / math.sqrt(hd)
    me = lax.axis_index("seq")
    copies = [
        pltpu.make_async_copy(out_in, out_ref, sems.at[0]),
        pltpu.make_async_copy(dq_in, dq_ref, sems.at[1]),
    ]
    for copy in copies:
        copy.start()
    dk_ref[:, 0:hd] = dkw_ref[...]
    dv_ref[:, 0:hd] = dvw_ref[...]
    join(near_ref, far_ref, stats)
    query_at = lax.broadcasted_iota(jnp.int32, (g, CLUS), 1)
    key_at = lax.broadcasted_iota(jnp.int32, (g, CLUS), 0)

    def step(k, carry):
        m = chunk_of(cfg, tab, me, k)
        first = m & ~(shards - 1)
        rank = (m & (shards - 1)) * g
        mine = aligned(k, g)
        whole = aligned(m >> log2(shards), CLUS)
        top, delta = [], []
        for j in range(shards):
            at = (tab[first + j] ^ me) * 2 * shards + tab[cfg["chunks"] + first + j]
            top.append(stats[pl.ds(at, 1), 0:g])
            delta.append(stats[pl.ds(at + shards, 1), 0:g])
        allowed = query_at >= key_at + rank
        p = jnp.exp(jnp.where(allowed, s_ref[mine, :] - jnp.concatenate(top, axis=1), NEG))
        ds = p * (dp_ref[mine, :] - jnp.concatenate(delta, axis=1)) * scale
        outs[mine, 0:hd] = dot(ds.astype(BF16), rows_ref[whole, 0:hd]).astype(BF16)
        outs[mine, hd:] = dot(p.astype(BF16), rows_ref[whole, hd:]).astype(BF16)
        return carry

    lax.fori_loop(0, shards, step, 0, unroll=min(shards, 8))
    back = dot(back_ref[...], outs[...]).astype(BF16)
    dk_ref[:, hd:] = back[:, 0:hd]
    dv_ref[:, hd:] = back[:, hd:]
    for copy in copies:
        copy.wait()


def partner(array, axis, mask):
    return lax.ppermute(array, axis, [(i, i ^ mask) for i in range(lax.axis_size(axis))])


def after(arrays, *earlier):
    return lax.optimization_barrier((arrays, earlier))[0]


def on_device(query_rows, key_rows, value_rows, out_grad, members):
    tok, width = query_rows.shape
    assert tok == WINDOW
    hd = width // 2
    shards = lax.axis_size("seq")
    heads = lax.axis_size("head")
    bits = log2(shards)
    me = lax.axis_index("seq")
    per = members.shape[0]
    total = per * shards * heads
    g = CLUS // shards
    cfg = dict(
        shards=shards, heads=heads, tok=tok, hd=hd, per=per, g=g, chunks=total // g, per_row=per // g
    )
    big = 2 if shards <= 8 else 4
    full = shape(tok, width)
    sides = [query_rows, key_rows, value_rows, out_grad]
    evens = list(range(2, shards, 2))

    kv_c, qg_c, kv_w, qg_w, *pieces, both, rim, spread = call(
        functools.partial(payloads, bits, hd),
        [full] * (bits + 3) + [shape(tok, 3 * width), full, shape(shards * heads, per, dtype=jnp.int32)],
        [pltpu.with_memory_space_constraint(x, pltpu.HBM) for x in [members.reshape(1, per)] + sides],
        scratch=[
            pltpu.VMEM((1, per), jnp.int32),
            pltpu.VMEM((shards * heads, per), jnp.int32),
            pltpu.SemaphoreType.DMA((10,)),
        ],
        hbm_outs=(bits + 5,),
        anywhere=(0, 1, 2, 3, 4),
        vmem=6 + bits,
    )
    got = {mask: partner(pieces[mask.bit_length() - 2], "seq", mask) for mask in evens}
    got[1] = partner(both, "seq", 1)
    lists = lax.all_to_all(after(spread, got[1]), ("seq", "head"), 0, 0, tiled=True)
    crossing = [(i, i + 1) for i in range(1, shards - 1, 2)] + [(shards - 1, 0)]
    crossing += [(b, a) for a, b in crossing]
    far = lax.ppermute(after(rim, lists), "seq", crossing)
    for mask in evens:
        got[mask + 1] = partner(after(got[mask], lists), "seq", 1)

    table = 3 * (total // g)
    rows_shape = shape(total, 2 * hd)
    stat = shape(2 * shards, LANES, dtype=F32)
    rows, qg, kv, back, p, ds, st_c, tab = call(
        functools.partial(sort_and_score, cfg),
        [rows_shape, full, full, shape(tok, tok), shape(tok, CLUS), shape(tok, CLUS), stat, shape(table, dtype=jnp.int32)],
        [lists, kv_c, qg_c] + [got[mask] for mask in range(1, shards)],
        scratch=[
            pltpu.SMEM((shards * heads, per), jnp.int32),
            pltpu.SMEM((table,), jnp.int32),
            pltpu.SMEM((shards,), jnp.int32),
            pltpu.SemaphoreType.DMA((2,)),
            pltpu.VMEM((total, LANES), F32),
            pltpu.VMEM((2, tok, tok), BF16),
            pltpu.VMEM((2, tok, 2 * hd), BF16),
        ],
        us=5.0,
        vmem=12 * big,
    )
    tile = 256
    def gather_step(held, bit, *earlier):
        return held, partner(after(held, *earlier), "seq", 1 << bit)

    def joined(held, other):
        rows_of = held.shape[0]
        return call(join, [shape(2 * rows_of, LANES, dtype=F32)], [held, other], vmem=2)[0]

    held, other = gather_step(st_c, 0)
    scored = shape(tok, CLUS, dtype=F32)
    rows, outs, s, dp = call(
        functools.partial(finish_queries, cfg),
        [rows_shape, full, scored, scored],
        [tab, rows, p, ds, qg, kv],
        smem=(0,),
        us=2.0,
        aliases={1: 0},
        vmem=6 * big,
    )
    for bit in range(1, bits - 1):
        held, other = gather_step(joined(held, after(other, outs)), bit)
    window = shape(tok, tok + tile)
    longer = shape(2 * tok, hd)
    p_w, ds_w, st_w, kx, vx = call(
        functools.partial(window_scores, tok, hd, tile),
        [window, window, shape(8, tok, dtype=F32), longer, longer],
        [after(kv_w, outs, held), qg_w, got[1], far],
        us=1.3,
        vmem=8,
    )
    near_st = partner(st_w, "seq", 1)
    far_st = lax.ppermute(st_w, "seq", crossing)
    held, other = gather_step(joined(held, after(other, st_w)), bits - 1)
    out_all, dq_all = call(
        functools.partial(query_outputs, tok, hd, tile),
        [full, full],
        [p_w, ds_w, kx, vx, back, outs],
        us=0.2,
        vmem=8,
    )
    dk_w, dv_w = call(
        functools.partial(window_keys, tok, hd, tile),
        [shape(tok, hd)] * 2,
        [kv_w, qg_w, got[1], far, after(st_w, out_all), near_st, far_st],
        scratch=[pltpu.VMEM((2 * tok, hd), BF16)] * 2 + [pltpu.VMEM((8, 2 * tok), F32)],
        us=0.2,
        vmem=8,
    )
    return call(
        functools.partial(key_outputs, cfg),
        [full] * 4,
        [tab, rows, back, s, dp, held, other, out_all, dq_all, dk_w, dv_w],
        scratch=[
            pltpu.VMEM((2 * shards * shards, LANES), F32),
            pltpu.VMEM((tok, 2 * hd), BF16),
            pltpu.SemaphoreType.DMA((2,)),
        ],
        smem=(0,),
        hbm_outs=(0, 1),
        us=2.6,
        vmem=4 * big,
    )


def solution(mesh):
    rows = P("seq", "head")
    return jax.shard_map(
        on_device,
        mesh=mesh,
        in_specs=(rows, rows, rows, rows, P(("seq", "head"))),
        out_specs=(rows, rows, rows, rows),
        check_vma=False,
    )
```

```python
import functools
import math

import jax
import jax.numpy as jnp
from jax import lax
from jax.experimental import pallas as pl
from jax.experimental.pallas import tpu as pltpu
from jax.sharding import PartitionSpec as P

CLUS = 512
WINDOW = 512
F32 = jnp.float32
BF16 = jnp.bfloat16
NEG = -1e30
LANES = 128

NN = (((1,), (0,)), ((), ()))
NT = (((1,), (1,)), ((), ()))


def dot(left, right, dims=NN):
    return lax.dot_general(left, right, dims, preferred_element_type=F32)


def call(body, outs, inputs, scratch=(), smem=(), hbm_outs=(), anywhere=(), us=0.0, aliases=None, vmem=8):
    def space(i, scalar):
        if i in scalar:
            return pltpu.SMEM
        return pl.ANY if i in anywhere else pltpu.VMEM

    moved = sum(x.size * x.dtype.itemsize for x in list(inputs) + list(outs))
    return pl.pallas_call(
        body,
        out_shape=outs,
        in_specs=[pl.BlockSpec(memory_space=space(i, smem)) for i in range(len(inputs))],
        out_specs=[
            pl.BlockSpec(memory_space=pl.ANY if i in hbm_outs else pltpu.VMEM) for i in range(len(outs))
        ],
        scratch_shapes=list(scratch),
        input_output_aliases=aliases or {},
        compiler_params=pltpu.CompilerParams(vmem_limit_bytes=vmem * 1024 * 1024),
        cost_estimate=pl.CostEstimate(flops=int(us * 1.15e9), bytes_accessed=moved, transcendentals=0),
    )(*inputs)


def shape(*dims, dtype=BF16):
    return jax.ShapeDtypeStruct(dims, dtype)


def to_row(column):
    n = column.shape[0]
    same = lax.broadcasted_iota(jnp.int32, (n, n), 0) == lax.broadcasted_iota(jnp.int32, (n, n), 1)
    return jnp.sum(jnp.where(same, column, 0.0), axis=0, keepdims=True)


def aligned(index, size):
    return pl.ds(pl.multiple_of(index * size, size), size)


def payloads(bits, hd, members_ref, q, k, v, g, *refs):
    kv_c, qg_c, kv_w, qg_w = refs[:4]
    pieces, (both, rim, spread, entries, repeated, sems) = refs[4 : 3 + bits], refs[3 + bits :]
    me = lax.axis_index("seq")
    width = 2 * hd
    copies = [pltpu.make_async_copy(members_ref, entries, sems.at[8])]
    for i, (source, target, lo, at) in enumerate(
        (
            (k, kv_c, hd, 0),
            (v, kv_c, hd, hd),
            (q, qg_c, hd, 0),
            (g, qg_c, hd, hd),
            (k, kv_w, 0, 0),
            (v, kv_w, 0, hd),
            (q, qg_w, 0, 0),
            (g, qg_w, 0, hd),
        )
    ):
        copies.append(
            pltpu.make_async_copy(source.at[:, lo : lo + hd], target.at[:, at : at + hd], sems.at[i])
        )
    for copy in copies:
        copy.start()
    copies[0].wait()
    repeated[...] = jnp.broadcast_to(entries[...], repeated.shape)
    copies.append(pltpu.make_async_copy(repeated, spread, sems.at[9]))
    copies[-1].start()
    for copy in copies[1:5]:
        copy.wait()

    def choose(bit, target, zero, one):
        low = ((me >> bit) & 1) == 0

        @pl.when(low)
        def _():
            target[:, 0:width] = zero[...]

        @pl.when(jnp.logical_not(low))
        def _():
            target[:, 0:width] = one[...]

    for bit in range(1, bits):
        choose(bit, pieces[bit - 1], kv_c, qg_c)
    choose(0, both, kv_c, qg_c)
    for copy in copies[5:]:
        copy.wait()
    choose(0, rim, qg_w, kv_w)
    both[:, width : 2 * width] = kv_w[...]
    both[:, 2 * width :] = qg_w[...]


def neighbour(parity, near_ref, block, far_ref, targets, at):
    tok, width = far_ref.shape
    hd = width // 2
    near = (lax.axis_index("seq") & 1) == parity

    @pl.when(near)
    def _():
        for i, target in enumerate(targets):
            lo = block * width + i * hd
            target[at : at + tok] = near_ref[:, lo : lo + hd]

    @pl.when(jnp.logical_not(near))
    def _():
        for i, target in enumerate(targets):
            target[at : at + tok] = far_ref[:, i * hd : (i + 1) * hd]


def window_rows(q, g, keys, values, allowed, scale):
    s = jnp.where(allowed, dot(q, keys, NT) * scale, NEG)
    dp = dot(g, values, NT)
    top = jnp.max(s, axis=1, keepdims=True)
    e = jnp.exp(s - top)
    total = jnp.sum(e, axis=1, keepdims=True)
    p = e * (1.0 / total)
    delta = jnp.sum(p * dp, axis=1, keepdims=True)
    return p, dp, to_row(top + jnp.log(total)), to_row(delta)


def window_scores(tok, hd, tile, *refs):
    kv_ref, qg_ref, near_ref, far_ref, p_ref, ds_ref, st_ref, kx, vx = refs
    scale = 1.0 / math.sqrt(hd)
    neighbour(1, near_ref, 1, far_ref, (kx, vx), 0)
    kx[tok:] = kv_ref[:, 0:hd]
    vx[tok:] = kv_ref[:, hd:]
    first = jnp.where(lax.axis_index("seq") == 0, tok, 0)
    span = tok + tile
    row = lax.broadcasted_iota(jnp.int32, (tile, span), 0)
    col = lax.broadcasted_iota(jnp.int32, (tile, span), 1)
    for lo in range(0, tok, tile):
        here = slice(lo, lo + tile)
        allowed = (col > row) & (col <= row + tok) & (col + lo >= first)
        s = jnp.where(allowed, dot(qg_ref[here, 0:hd], kx[lo : lo + span], NT) * scale, NEG)
        dp = dot(qg_ref[here, hd:], vx[lo : lo + span], NT)
        top = jnp.max(s, axis=1, keepdims=True)
        e = jnp.exp(s - top)
        total = jnp.sum(e, axis=1, keepdims=True)
        p = e * (1.0 / total)
        delta = jnp.sum(p * dp, axis=1, keepdims=True)
        p_ref[here, :] = p.astype(BF16)
        ds_ref[here, :] = (p * (dp - delta) * scale).astype(BF16)
        st_ref[0:1, here] = to_row(top + jnp.log(total))
        st_ref[1:2, here] = to_row(delta)


def query_outputs(tok, hd, tile, *refs):
    p_ref, ds_ref, kx, vx, back_ref, outs_ref = refs[:6]
    out_ref, dq_ref = refs[10:12]
    span = tok + tile
    for lo in range(0, tok, tile):
        here = slice(lo, lo + tile)
        out_ref[here, 0:hd] = dot(p_ref[here, :], vx[lo : lo + span]).astype(BF16)
        dq_ref[here, 0:hd] = dot(ds_ref[here, :], kx[lo : lo + span]).astype(BF16)
    back = dot(back_ref[...], outs_ref[...]).astype(BF16)
    out_ref[:, hd:] = back[:, 0:hd]
    dq_ref[:, hd:] = back[:, hd:]
    window_key_scores(tok, hd, tile, *refs[6:10], *refs[12:])


def window_key_scores(tok, hd, tile, kv_ref, qg_ref, near_ref, far_ref, s_ref, dp_ref, qx, gx):
    scale = 1.0 / math.sqrt(hd)
    neighbour(0, near_ref, 2, far_ref, (qx, gx), tok)
    qx[0:tok] = qg_ref[:, 0:hd]
    gx[0:tok] = qg_ref[:, hd:]
    last = jnp.where(lax.axis_index("seq") == lax.axis_size("seq") - 1, tok, 2 * tok)
    span = tok + tile
    row = lax.broadcasted_iota(jnp.int32, (tile, span), 0)
    col = lax.broadcasted_iota(jnp.int32, (tile, span), 1)
    for lo in range(0, tok, tile):
        here = slice(lo, lo + tile)
        allowed = (col >= row) & (col < row + tok) & (col + lo < last)
        s = dot(kv_ref[here, 0:hd], qx[lo : lo + span], NT) * scale
        s_ref[here, :] = jnp.where(allowed, s, NEG)
        dp_ref[here, :] = dot(kv_ref[here, hd:], gx[lo : lo + span], NT)


def window_keys(tok, hd, tile, s_ref, dp_ref, qx, gx, st_ref, next_ref, dk_ref, dv_ref, stx):
    scale = 1.0 / math.sqrt(hd)
    stx[:, 0:tok] = st_ref[...]
    stx[:, tok:] = next_ref[...]
    span = tok + tile
    for lo in range(0, tok, tile):
        here = slice(lo, lo + tile)
        p = jnp.exp(s_ref[here, :] - stx[0:1, lo : lo + span])
        dv_ref[here, 0:hd] = dot(p.astype(BF16), gx[lo : lo + span]).astype(BF16)
        ds = (p * (dp_ref[here, :] - stx[1:2, lo : lo + span]) * scale).astype(BF16)
        dk_ref[here, 0:hd] = dot(ds, qx[lo : lo + span]).astype(BF16)


def log2(n):
    return n.bit_length() - 1


def make_tables(cfg, lists_smem, tab, count):
    shards, g, tok, chunks = cfg["shards"], cfg["g"], cfg["tok"], cfg["chunks"]
    for s in range(shards):
        count[s] = 0

    def step(m, carry):
        s = lists_smem[m >> log2(cfg["per_row"]), (m & (cfg["per_row"] - 1)) * g] >> log2(tok)
        pos = count[s]
        count[s] = pos + 1
        tab[m] = s
        tab[chunks + m] = pos
        tab[2 * chunks + s * shards + pos] = m
        return carry

    lax.fori_loop(0, chunks, step, 0, unroll=min(chunks, 64))


def chunk_of(cfg, tab, s, k):
    return tab[2 * cfg["chunks"] + s * cfg["shards"] + k]


def make_columns(cfg, lists_ref, columns):
    tok, per = cfg["tok"], cfg["per"]
    same = lax.broadcasted_iota(jnp.int32, (per, per), 0) == lax.broadcasted_iota(jnp.int32, (per, per), 1)
    rows = lists_ref.shape[0]

    def step(r, carry):
        row = (lists_ref[pl.ds(r, 1), :] & (tok - 1)).astype(F32)
        columns[aligned(r, per), 0:1] = jnp.sum(jnp.where(same, row, 0.0), axis=1, keepdims=True)
        return carry

    lax.fori_loop(0, rows, step, 0, unroll=min(rows, 32))


def build_order(cfg, columns, tab, s, order_ref):
    shards, g, tok = cfg["shards"], cfg["g"], cfg["tok"]
    token = lax.broadcasted_iota(jnp.int32, (g, tok), 1).astype(F32)

    def step(k, carry):
        column = columns[aligned(chunk_of(cfg, tab, s, k), g), 0:1]
        order_ref[aligned(k, g), :] = jnp.where(column == token, 1.0, 0.0).astype(BF16)
        return carry

    lax.fori_loop(0, shards, step, 0, unroll=min(shards, 8))


def place(cfg, tab, s, rows_ref, to_ref):
    shards, g = cfg["shards"], cfg["g"]

    def step(k, carry):
        m = chunk_of(cfg, tab, s, k)
        to_ref[aligned(m, g), :] = rows_ref[aligned(k, g), :]
        return carry

    lax.fori_loop(0, shards, step, 0, unroll=min(shards, 8))


def sort_blocks(cfg, columns, tab, masks, arrived, rows_ref, orders, sorted_rows):
    for i, (mask, block) in enumerate(zip(masks, arrived)):
        s = lax.axis_index("seq") ^ mask
        order, rows = orders.at[i % 2], sorted_rows.at[i % 2]
        build_order(cfg, columns, tab, s, order)
        rows[...] = dot(order[...], block[:, 0 : rows.shape[1]]).astype(BF16)
        place(cfg, tab, s, rows, rows_ref)


def sort_and_score(cfg, *refs):
    shards, g, hd = cfg["shards"], cfg["g"], cfg["hd"]
    (lists_ref, kv_in, qg_in), refs = refs[:3], refs[3:]
    arrived, refs = refs[: shards - 1], refs[shards - 1 :]
    rows_ref, qg_ref, kv_ref, back_ref, p_ref, ds_ref, st_ref, tab_out = refs[:8]
    lists_smem, tab, count, sems, columns, orders, sorted_rows = refs[8:]
    scale = 1.0 / math.sqrt(hd)
    me = lax.axis_index("seq")
    load = pltpu.make_async_copy(lists_ref, lists_smem, sems.at[0])
    load.start()
    make_columns(cfg, lists_ref, columns)
    load.wait()
    make_tables(cfg, lists_smem, tab, count)
    keep = pltpu.make_async_copy(tab, tab_out, sems.at[1])
    keep.start()
    build_order(cfg, columns, tab, me, orders.at[0])
    own = orders[0]
    back_ref[...] = jnp.transpose(own)
    qg_ref[...] = dot(own, qg_in[...]).astype(BF16)
    kv_ref[...] = dot(own, kv_in[...]).astype(BF16)
    place(cfg, tab, me, kv_ref, rows_ref)
    sort_blocks(cfg, columns, tab, range(1, shards), arrived, rows_ref, orders, sorted_rows)
    key_at = lax.broadcasted_iota(jnp.int32, (g, CLUS), 1)
    query_at = lax.broadcasted_iota(jnp.int32, (g, CLUS), 0)

    def step(k, carry):
        m = chunk_of(cfg, tab, me, k)
        rank = (m & (shards - 1)) * g
        mine = aligned(k, g)
        whole = aligned(m >> log2(shards), CLUS)
        s = dot(qg_ref[mine, 0:hd], rows_ref[whole, 0:hd], NT) * scale
        dp = dot(qg_ref[mine, hd:], rows_ref[whole, hd:], NT)
        s = jnp.where(key_at <= query_at + rank, s, NEG)
        top = jnp.max(s, axis=1, keepdims=True)
        e = jnp.exp(s - top)
        total = jnp.sum(e, axis=1, keepdims=True)
        p = e * (1.0 / total)
        delta = jnp.sum(p * dp, axis=1, keepdims=True)
        p_ref[mine, :] = p.astype(BF16)
        ds_ref[mine, :] = (p * (dp - delta) * scale).astype(BF16)
        st_ref[pl.ds(k, 1), 0:g] = to_row(top + jnp.log(total))
        st_ref[pl.ds(shards + k, 1), 0:g] = to_row(delta)
        return carry

    lax.fori_loop(0, shards, step, 0, unroll=min(shards, 8))
    keep.wait()


def join(own_ref, other_ref, out_ref):
    rows = own_ref.shape[0]
    out_ref[0:rows] = own_ref[...]
    out_ref[rows:] = other_ref[...]


def finish_queries(cfg, *refs):
    shards, g, hd = cfg["shards"], cfg["g"], cfg["hd"]
    tab, rows_in, p_ref, ds_ref, qg_ref, kv_ref, rows_ref, outs, s_ref, dp_ref = refs
    del rows_in
    scale = 1.0 / math.sqrt(hd)
    me = lax.axis_index("seq")

    def query_step(k, carry):
        mine = aligned(k, g)
        whole = aligned(chunk_of(cfg, tab, me, k) >> log2(shards), CLUS)
        outs[mine, 0:hd] = dot(p_ref[mine, :], rows_ref[whole, hd:]).astype(BF16)
        outs[mine, hd:] = dot(ds_ref[mine, :], rows_ref[whole, 0:hd]).astype(BF16)
        return carry

    lax.fori_loop(0, shards, query_step, 0, unroll=min(shards, 8))
    place(cfg, tab, me, qg_ref, rows_ref)

    def key_step(k, carry):
        mine = aligned(k, g)
        whole = aligned(chunk_of(cfg, tab, me, k) >> log2(shards), CLUS)
        s_ref[mine, :] = dot(kv_ref[mine, 0:hd], rows_ref[whole, 0:hd], NT) * scale
        dp_ref[mine, :] = dot(kv_ref[mine, hd:], rows_ref[whole, hd:], NT)
        return carry

    lax.fori_loop(0, shards, key_step, 0, unroll=min(shards, 8))


def key_outputs(cfg, tile, *refs):
    shards, g, hd = cfg["shards"], cfg["g"], cfg["hd"]
    (tab_ref, rows_ref, back_ref, s_ref, dp_ref, near_ref, far_ref, out_in, dq_in), refs = refs[:9], refs[9:]
    window, (out_ref, dq_ref, dk_ref, dv_ref), refs = refs[:6], refs[6:10], refs[10:]
    tab, stats, outs, sems = refs[:4]
    scale = 1.0 / math.sqrt(hd)
    me = lax.axis_index("seq")
    copies = [
        pltpu.make_async_copy(out_in, out_ref, sems.at[0]),
        pltpu.make_async_copy(dq_in, dq_ref, sems.at[1]),
    ]
    load = pltpu.make_async_copy(tab_ref, tab, sems.at[2])
    load.start()
    for copy in copies:
        copy.start()
    window_keys(cfg["tok"], hd, tile, *window, dk_ref, dv_ref, *refs[4:])
    load.wait()
    join(near_ref, far_ref, stats)
    query_at = lax.broadcasted_iota(jnp.int32, (g, CLUS), 1)
    key_at = lax.broadcasted_iota(jnp.int32, (g, CLUS), 0)

    def step(k, carry):
        m = chunk_of(cfg, tab, me, k)
        first = m & ~(shards - 1)
        rank = (m & (shards - 1)) * g
        mine = aligned(k, g)
        whole = aligned(m >> log2(shards), CLUS)
        top, delta = [], []
        for j in range(shards):
            at = (tab[first + j] ^ me) * 2 * shards + tab[cfg["chunks"] + first + j]
            top.append(stats[pl.ds(at, 1), 0:g])
            delta.append(stats[pl.ds(at + shards, 1), 0:g])
        allowed = query_at >= key_at + rank
        p = jnp.exp(jnp.where(allowed, s_ref[mine, :] - jnp.concatenate(top, axis=1), NEG))
        ds = p * (dp_ref[mine, :] - jnp.concatenate(delta, axis=1)) * scale
        outs[mine, 0:hd] = dot(ds.astype(BF16), rows_ref[whole, 0:hd]).astype(BF16)
        outs[mine, hd:] = dot(p.astype(BF16), rows_ref[whole, hd:]).astype(BF16)
        return carry

    lax.fori_loop(0, shards, step, 0, unroll=min(shards, 8))
    back = dot(back_ref[...], outs[...]).astype(BF16)
    dk_ref[:, hd:] = back[:, 0:hd]
    dv_ref[:, hd:] = back[:, hd:]
    for copy in copies:
        copy.wait()


def partner(array, axis, mask):
    return lax.ppermute(array, axis, [(i, i ^ mask) for i in range(lax.axis_size(axis))])


def after(arrays, *earlier):
    return lax.optimization_barrier((arrays, earlier))[0]


def on_device(query_rows, key_rows, value_rows, out_grad, members):
    tok, width = query_rows.shape
    assert tok == WINDOW
    hd = width // 2
    shards = lax.axis_size("seq")
    heads = lax.axis_size("head")
    bits = log2(shards)
    me = lax.axis_index("seq")
    per = members.shape[0]
    total = per * shards * heads
    g = CLUS // shards
    cfg = dict(
        shards=shards, heads=heads, tok=tok, hd=hd, per=per, g=g, chunks=total // g, per_row=per // g
    )
    big = 2 if shards <= 8 else 4
    full = shape(tok, width)
    sides = [query_rows, key_rows, value_rows, out_grad]
    evens = list(range(2, shards, 2))

    kv_c, qg_c, kv_w, qg_w, *pieces, both, rim, spread = call(
        functools.partial(payloads, bits, hd),
        [full] * (bits + 3) + [shape(tok, 3 * width), full, shape(shards * heads, per, dtype=jnp.int32)],
        [pltpu.with_memory_space_constraint(x, pltpu.HBM) for x in [members.reshape(1, per)] + sides],
        scratch=[
            pltpu.VMEM((1, per), jnp.int32),
            pltpu.VMEM((shards * heads, per), jnp.int32),
            pltpu.SemaphoreType.DMA((10,)),
        ],
        hbm_outs=(bits + 5,),
        anywhere=(0, 1, 2, 3, 4),
        vmem=6 + bits,
    )
    got = {mask: partner(pieces[mask.bit_length() - 2], "seq", mask) for mask in evens}
    got[1] = partner(both, "seq", 1)
    lists = lax.all_to_all(after(spread, got[1]), ("seq", "head"), 0, 0, tiled=True)
    crossing = [(i, i + 1) for i in range(1, shards - 1, 2)] + [(shards - 1, 0)]
    crossing += [(b, a) for a, b in crossing]
    far = lax.ppermute(after(rim, lists), "seq", crossing)
    for mask in evens:
        got[mask + 1] = partner(after(got[mask], lists), "seq", 1)

    table = 3 * (total // g)
    rows_shape = shape(total, 2 * hd)
    stat = shape(2 * shards, LANES, dtype=F32)
    rows, qg, kv, back, p, ds, st_c, tab = call(
        functools.partial(sort_and_score, cfg),
        [rows_shape, full, full, shape(tok, tok), shape(tok, CLUS), shape(tok, CLUS), stat, shape(table, dtype=jnp.int32)],
        [lists, kv_c, qg_c] + [got[mask] for mask in range(1, shards)],
        scratch=[
            pltpu.SMEM((shards * heads, per), jnp.int32),
            pltpu.SMEM((table,), jnp.int32),
            pltpu.SMEM((shards,), jnp.int32),
            pltpu.SemaphoreType.DMA((2,)),
            pltpu.VMEM((total, LANES), F32),
            pltpu.VMEM((2, tok, tok), BF16),
            pltpu.VMEM((2, tok, 2 * hd), BF16),
        ],
        us=5.0,
        vmem=12 * big,
    )
    tile = 256
    def gather_step(held, bit, *earlier):
        return held, partner(after(held, *earlier), "seq", 1 << bit)

    def joined(held, other):
        rows_of = held.shape[0]
        return call(join, [shape(2 * rows_of, LANES, dtype=F32)], [held, other], vmem=2)[0]

    other, beyond = partner(st_c, "seq", 1), partner(st_c, "seq", 2)
    scored = shape(tok, CLUS, dtype=F32)
    rows, outs, s, dp = call(
        functools.partial(finish_queries, cfg),
        [rows_shape, full, scored, scored],
        [tab, rows, p, ds, qg, kv],
        smem=(0,),
        us=2.0,
        aliases={1: 0},
        vmem=6 * big,
    )
    behind = partner(after(beyond, outs), "seq", 1)
    window = shape(tok, tok + tile)
    longer = shape(2 * tok, hd)
    p_w, ds_w, st_w, kx, vx = call(
        functools.partial(window_scores, tok, hd, tile),
        [window, window, shape(8, tok, dtype=F32), longer, longer],
        [after(kv_w, outs), qg_w, got[1], far],
        us=1.3,
        vmem=8,
    )
    held, other = joined(st_c, other), joined(beyond, after(behind, st_w))
    for bit in range(2, bits):
        held, other = gather_step(joined(held, other), bit)
    st_next = lax.ppermute(st_w, "seq", [((i + 1) % shards, i) for i in range(shards)])
    scores = shape(tok, tok + tile, dtype=F32)
    out_all, dq_all, s_w, dp_w, qx, gx = call(
        functools.partial(query_outputs, tok, hd, tile),
        [full, full, scores, scores, longer, longer],
        [p_w, ds_w, kx, vx, back, outs, kv_w, qg_w, got[1], far],
        us=0.2,
        vmem=12,
    )
    return call(
        functools.partial(key_outputs, cfg, tile),
        [full] * 4,
        [tab, rows, back, s, dp, held, other, out_all, dq_all, s_w, dp_w, qx, gx, st_w, st_next],
        scratch=[
            pltpu.SMEM((table,), jnp.int32),
            pltpu.VMEM((2 * shards * shards, LANES), F32),
            pltpu.VMEM((tok, 2 * hd), BF16),
            pltpu.SemaphoreType.DMA((3,)),
            pltpu.VMEM((8, 2 * tok), F32),
        ],
        hbm_outs=(0, 1),
        us=3.3,
        vmem=5 * big,
    )


def solution(mesh):
    rows = P("seq", "head")
    return jax.shard_map(
        on_device,
        mesh=mesh,
        in_specs=(rows, rows, rows, rows, P(("seq", "head"))),
        out_specs=(rows, rows, rows, rows),
        check_vma=False,
    )
```

```python
import functools
import math

import jax
import jax.numpy as jnp
from jax import lax
from jax.experimental import pallas as pl
from jax.experimental.pallas import tpu as pltpu
from jax.sharding import PartitionSpec as P

CLUS = 512
WINDOW = 512
F32 = jnp.float32
BF16 = jnp.bfloat16
NEG = -1e30
LANES = 128

NN = (((1,), (0,)), ((), ()))
NT = (((1,), (1,)), ((), ()))


def dot(left, right, dims=NN):
    return lax.dot_general(left, right, dims, preferred_element_type=F32)


def call(body, outs, inputs, scratch=(), smem=(), hbm_outs=(), anywhere=(), us=0.0, aliases=None, vmem=8):
    def space(i, scalar):
        if i in scalar:
            return pltpu.SMEM
        return pl.ANY if i in anywhere else pltpu.VMEM

    moved = sum(x.size * x.dtype.itemsize for x in list(inputs) + list(outs))
    return pl.pallas_call(
        body,
        out_shape=outs,
        in_specs=[pl.BlockSpec(memory_space=space(i, smem)) for i in range(len(inputs))],
        out_specs=[
            pl.BlockSpec(memory_space=pl.ANY if i in hbm_outs else pltpu.VMEM) for i in range(len(outs))
        ],
        scratch_shapes=list(scratch),
        input_output_aliases=aliases or {},
        compiler_params=pltpu.CompilerParams(vmem_limit_bytes=vmem * 1024 * 1024),
        cost_estimate=pl.CostEstimate(flops=int(us * 1.15e9), bytes_accessed=moved, transcendentals=0),
    )(*inputs)


def shape(*dims, dtype=BF16):
    return jax.ShapeDtypeStruct(dims, dtype)


def to_row(column):
    n = column.shape[0]
    same = lax.broadcasted_iota(jnp.int32, (n, n), 0) == lax.broadcasted_iota(jnp.int32, (n, n), 1)
    return jnp.sum(jnp.where(same, column, 0.0), axis=0, keepdims=True)


def aligned(index, size):
    return pl.ds(pl.multiple_of(index * size, size), size)


def payloads(bits, hd, members_ref, q, k, v, g, *refs):
    kv_c, qg_c, kv_w, qg_w = refs[:4]
    pieces, (both, rim, spread, entries, repeated, sems) = refs[4 : 3 + bits], refs[3 + bits :]
    me = lax.axis_index("seq")
    width = 2 * hd
    copies = [pltpu.make_async_copy(members_ref, entries, sems.at[8])]
    for i, (source, target, lo, at) in enumerate(
        (
            (k, kv_c, hd, 0),
            (v, kv_c, hd, hd),
            (q, qg_c, hd, 0),
            (g, qg_c, hd, hd),
            (k, kv_w, 0, 0),
            (v, kv_w, 0, hd),
            (q, qg_w, 0, 0),
            (g, qg_w, 0, hd),
        )
    ):
        copies.append(
            pltpu.make_async_copy(source.at[:, lo : lo + hd], target.at[:, at : at + hd], sems.at[i])
        )
    for copy in copies:
        copy.start()
    copies[0].wait()
    repeated[...] = jnp.broadcast_to(entries[...], repeated.shape)
    copies.append(pltpu.make_async_copy(repeated, spread, sems.at[9]))
    copies[-1].start()
    for copy in copies[1:5]:
        copy.wait()

    def choose(bit, target, zero, one):
        low = ((me >> bit) & 1) == 0

        @pl.when(low)
        def _():
            target[:, 0:width] = zero[...]

        @pl.when(jnp.logical_not(low))
        def _():
            target[:, 0:width] = one[...]

    for bit in range(1, bits):
        choose(bit, pieces[bit - 1], kv_c, qg_c)
    choose(0, both, kv_c, qg_c)
    for copy in copies[5:]:
        copy.wait()
    choose(0, rim, qg_w, kv_w)
    both[:, width : 2 * width] = kv_w[...]
    both[:, 2 * width :] = qg_w[...]


def neighbour(parity, near_ref, block, far_ref, targets, at):
    tok, width = far_ref.shape
    hd = width // 2
    near = (lax.axis_index("seq") & 1) == parity

    @pl.when(near)
    def _():
        for i, target in enumerate(targets):
            lo = block * width + i * hd
            target[at : at + tok] = near_ref[:, lo : lo + hd]

    @pl.when(jnp.logical_not(near))
    def _():
        for i, target in enumerate(targets):
            target[at : at + tok] = far_ref[:, i * hd : (i + 1) * hd]


def window_rows(q, g, keys, values, allowed, scale):
    s = jnp.where(allowed, dot(q, keys, NT) * scale, NEG)
    dp = dot(g, values, NT)
    top = jnp.max(s, axis=1, keepdims=True)
    e = jnp.exp(s - top)
    total = jnp.sum(e, axis=1, keepdims=True)
    p = e * (1.0 / total)
    delta = jnp.sum(p * dp, axis=1, keepdims=True)
    return p, dp, to_row(top + jnp.log(total)), to_row(delta)


def window_scores(tok, hd, tile, *refs):
    kv_ref, qg_ref, near_ref, far_ref, p_ref, ds_ref, st_ref, kx, vx = refs
    scale = 1.0 / math.sqrt(hd)
    neighbour(1, near_ref, 1, far_ref, (kx, vx), 0)
    kx[tok:] = kv_ref[:, 0:hd]
    vx[tok:] = kv_ref[:, hd:]
    first = jnp.where(lax.axis_index("seq") == 0, tok, 0)
    span = tok + tile
    row = lax.broadcasted_iota(jnp.int32, (tile, span), 0)
    col = lax.broadcasted_iota(jnp.int32, (tile, span), 1)
    for lo in range(0, tok, tile):
        here = slice(lo, lo + tile)
        allowed = (col > row) & (col <= row + tok) & (col + lo >= first)
        s = jnp.where(allowed, dot(qg_ref[here, 0:hd], kx[lo : lo + span], NT) * scale, NEG)
        dp = dot(qg_ref[here, hd:], vx[lo : lo + span], NT)
        top = jnp.max(s, axis=1, keepdims=True)
        e = jnp.exp(s - top)
        total = jnp.sum(e, axis=1, keepdims=True)
        p = e * (1.0 / total)
        delta = jnp.sum(p * dp, axis=1, keepdims=True)
        p_ref[here, :] = p.astype(BF16)
        ds_ref[here, :] = (p * (dp - delta) * scale).astype(BF16)
        st_ref[0:1, here] = to_row(top + jnp.log(total))
        st_ref[1:2, here] = to_row(delta)


def query_outputs(tok, hd, tile, *refs):
    p_ref, ds_ref, kx, vx, back_ref, outs_ref = refs[:6]
    out_ref, dq_ref = refs[10:12]
    span = tok + tile
    for lo in range(0, tok, tile):
        here = slice(lo, lo + tile)
        out_ref[here, 0:hd] = dot(p_ref[here, :], vx[lo : lo + span]).astype(BF16)
        dq_ref[here, 0:hd] = dot(ds_ref[here, :], kx[lo : lo + span]).astype(BF16)
    back = dot(back_ref[...], outs_ref[...]).astype(BF16)
    out_ref[:, hd:] = back[:, 0:hd]
    dq_ref[:, hd:] = back[:, hd:]
    window_key_scores(tok, hd, tile, *refs[6:10], *refs[12:])


def window_key_scores(tok, hd, tile, kv_ref, qg_ref, near_ref, far_ref, s_ref, dp_ref, qx, gx):
    scale = 1.0 / math.sqrt(hd)
    neighbour(0, near_ref, 2, far_ref, (qx, gx), tok)
    qx[0:tok] = qg_ref[:, 0:hd]
    gx[0:tok] = qg_ref[:, hd:]
    last = jnp.where(lax.axis_index("seq") == lax.axis_size("seq") - 1, tok, 2 * tok)
    span = tok + tile
    row = lax.broadcasted_iota(jnp.int32, (tile, span), 0)
    col = lax.broadcasted_iota(jnp.int32, (tile, span), 1)
    for lo in range(0, tok, tile):
        here = slice(lo, lo + tile)
        allowed = (col >= row) & (col < row + tok) & (col + lo < last)
        s = dot(kv_ref[here, 0:hd], qx[lo : lo + span], NT) * scale
        s_ref[here, :] = jnp.where(allowed, s, NEG)
        dp_ref[here, :] = dot(kv_ref[here, hd:], gx[lo : lo + span], NT)


def window_keys(tok, hd, tile, s_ref, dp_ref, qx, gx, st_ref, next_ref, dk_ref, dv_ref, stx):
    scale = 1.0 / math.sqrt(hd)
    stx[:, 0:tok] = st_ref[...]
    stx[:, tok:] = next_ref[...]
    span = tok + tile
    for lo in range(0, tok, tile):
        here = slice(lo, lo + tile)
        p = jnp.exp(s_ref[here, :] - stx[0:1, lo : lo + span])
        dv_ref[here, 0:hd] = dot(p.astype(BF16), gx[lo : lo + span]).astype(BF16)
        ds = (p * (dp_ref[here, :] - stx[1:2, lo : lo + span]) * scale).astype(BF16)
        dk_ref[here, 0:hd] = dot(ds, qx[lo : lo + span]).astype(BF16)


def log2(n):
    return n.bit_length() - 1


def make_tables(cfg, lists_smem, tab, count):
    shards, g, tok, chunks = cfg["shards"], cfg["g"], cfg["tok"], cfg["chunks"]
    for s in range(shards):
        count[s] = 0

    def step(m, carry):
        s = lists_smem[m >> log2(cfg["per_row"]), (m & (cfg["per_row"] - 1)) * g] >> log2(tok)
        pos = count[s]
        count[s] = pos + 1
        tab[m] = s
        tab[chunks + m] = pos
        tab[2 * chunks + s * shards + pos] = m
        return carry

    lax.fori_loop(0, chunks, step, 0, unroll=min(chunks, 64))


def chunk_of(cfg, tab, s, k):
    return tab[2 * cfg["chunks"] + s * cfg["shards"] + k]


def make_columns(cfg, lists_ref, columns):
    tok, per = cfg["tok"], cfg["per"]
    same = lax.broadcasted_iota(jnp.int32, (per, per), 0) == lax.broadcasted_iota(jnp.int32, (per, per), 1)
    rows = lists_ref.shape[0]

    def step(r, carry):
        row = (lists_ref[pl.ds(r, 1), :] & (tok - 1)).astype(F32)
        columns[aligned(r, per), 0:1] = jnp.sum(jnp.where(same, row, 0.0), axis=1, keepdims=True)
        return carry

    lax.fori_loop(0, rows, step, 0, unroll=min(rows, 32))


def build_order(cfg, columns, tab, s, order_ref):
    shards, g, tok = cfg["shards"], cfg["g"], cfg["tok"]
    token = lax.broadcasted_iota(jnp.int32, (g, tok), 1).astype(F32)

    def step(k, carry):
        column = columns[aligned(chunk_of(cfg, tab, s, k), g), 0:1]
        order_ref[aligned(k, g), :] = jnp.where(column == token, 1.0, 0.0).astype(BF16)
        return carry

    lax.fori_loop(0, shards, step, 0, unroll=min(shards, 8))


def place(cfg, tab, s, rows_ref, to_ref):
    shards, g = cfg["shards"], cfg["g"]

    def step(k, carry):
        m = chunk_of(cfg, tab, s, k)
        to_ref[aligned(m, g), :] = rows_ref[aligned(k, g), :]
        return carry

    lax.fori_loop(0, shards, step, 0, unroll=min(shards, 8))


def sort_blocks(cfg, columns, tab, masks, arrived, rows_ref, orders, sorted_rows):
    for i, (mask, block) in enumerate(zip(masks, arrived)):
        s = lax.axis_index("seq") ^ mask
        order, rows = orders.at[i % 2], sorted_rows.at[i % 2]
        build_order(cfg, columns, tab, s, order)
        rows[...] = dot(order[...], block[:, 0 : rows.shape[1]]).astype(BF16)
        place(cfg, tab, s, rows, rows_ref)


def sort_and_score(cfg, *refs):
    shards, g, hd = cfg["shards"], cfg["g"], cfg["hd"]
    (lists_ref, kv_in, qg_in), refs = refs[:3], refs[3:]
    arrived, refs = refs[: shards - 1], refs[shards - 1 :]
    rows_ref, qg_ref, kv_ref, back_ref, p_ref, ds_ref, st_ref, tab_out = refs[:8]
    lists_smem, tab, count, sems, columns, orders, sorted_rows = refs[8:]
    scale = 1.0 / math.sqrt(hd)
    me = lax.axis_index("seq")
    load = pltpu.make_async_copy(lists_ref, lists_smem, sems.at[0])
    load.start()
    make_columns(cfg, lists_ref, columns)
    load.wait()
    make_tables(cfg, lists_smem, tab, count)
    keep = pltpu.make_async_copy(tab, tab_out, sems.at[1])
    keep.start()
    build_order(cfg, columns, tab, me, orders.at[0])
    own = orders[0]
    back_ref[...] = jnp.transpose(own)
    qg_ref[...] = dot(own, qg_in[...]).astype(BF16)
    kv_ref[...] = dot(own, kv_in[...]).astype(BF16)
    place(cfg, tab, me, kv_ref, rows_ref)
    sort_blocks(cfg, columns, tab, range(1, shards), arrived, rows_ref, orders, sorted_rows)
    key_at = lax.broadcasted_iota(jnp.int32, (g, CLUS), 1)
    query_at = lax.broadcasted_iota(jnp.int32, (g, CLUS), 0)

    def step(k, carry):
        m = chunk_of(cfg, tab, me, k)
        rank = (m & (shards - 1)) * g
        mine = aligned(k, g)
        whole = aligned(m >> log2(shards), CLUS)
        s = dot(qg_ref[mine, 0:hd], rows_ref[whole, 0:hd], NT) * scale
        dp = dot(qg_ref[mine, hd:], rows_ref[whole, hd:], NT)
        s = jnp.where(key_at <= query_at + rank, s, NEG)
        top = jnp.max(s, axis=1, keepdims=True)
        e = jnp.exp(s - top)
        total = jnp.sum(e, axis=1, keepdims=True)
        p = e * (1.0 / total)
        delta = jnp.sum(p * dp, axis=1, keepdims=True)
        p_ref[mine, :] = p.astype(BF16)
        ds_ref[mine, :] = (p * (dp - delta) * scale).astype(BF16)
        st_ref[pl.ds(k, 1), 0:g] = to_row(top + jnp.log(total))
        st_ref[pl.ds(shards + k, 1), 0:g] = to_row(delta)
        return carry

    lax.fori_loop(0, shards, step, 0, unroll=min(shards, 8))
    keep.wait()


def join(own_ref, other_ref, out_ref):
    rows = own_ref.shape[0]
    out_ref[0:rows] = own_ref[...]
    out_ref[rows:] = other_ref[...]


def finish_queries(cfg, *refs):
    shards, g, hd = cfg["shards"], cfg["g"], cfg["hd"]
    tab, rows_in, p_ref, ds_ref, qg_ref, kv_ref, rows_ref, outs, s_ref, dp_ref = refs
    del rows_in
    scale = 1.0 / math.sqrt(hd)
    me = lax.axis_index("seq")

    def query_step(k, carry):
        mine = aligned(k, g)
        whole = aligned(chunk_of(cfg, tab, me, k) >> log2(shards), CLUS)
        outs[mine, 0:hd] = dot(p_ref[mine, :], rows_ref[whole, hd:]).astype(BF16)
        outs[mine, hd:] = dot(ds_ref[mine, :], rows_ref[whole, 0:hd]).astype(BF16)
        return carry

    lax.fori_loop(0, shards, query_step, 0, unroll=min(shards, 8))
    place(cfg, tab, me, qg_ref, rows_ref)

    def key_step(k, carry):
        mine = aligned(k, g)
        whole = aligned(chunk_of(cfg, tab, me, k) >> log2(shards), CLUS)
        s_ref[mine, :] = dot(kv_ref[mine, 0:hd], rows_ref[whole, 0:hd], NT) * scale
        dp_ref[mine, :] = dot(kv_ref[mine, hd:], rows_ref[whole, hd:], NT)
        return carry

    lax.fori_loop(0, shards, key_step, 0, unroll=min(shards, 8))


def key_outputs(cfg, tile, *refs):
    shards, g, hd = cfg["shards"], cfg["g"], cfg["hd"]
    (tab_ref, rows_ref, back_ref, s_ref, dp_ref, near_ref, far_ref, out_in, dq_in), refs = refs[:9], refs[9:]
    window, (out_ref, dq_ref, dk_ref, dv_ref), refs = refs[:6], refs[6:10], refs[10:]
    tab, stats, outs, sems = refs[:4]
    scale = 1.0 / math.sqrt(hd)
    me = lax.axis_index("seq")
    copies = [
        pltpu.make_async_copy(out_in, out_ref, sems.at[0]),
        pltpu.make_async_copy(dq_in, dq_ref, sems.at[1]),
    ]
    load = pltpu.make_async_copy(tab_ref, tab, sems.at[2])
    load.start()
    for copy in copies:
        copy.start()
    window_keys(cfg["tok"], hd, tile, *window, dk_ref, dv_ref, *refs[4:])
    load.wait()
    join(near_ref, far_ref, stats)
    query_at = lax.broadcasted_iota(jnp.int32, (g, CLUS), 1)
    key_at = lax.broadcasted_iota(jnp.int32, (g, CLUS), 0)

    def step(k, carry):
        m = chunk_of(cfg, tab, me, k)
        first = m & ~(shards - 1)
        rank = (m & (shards - 1)) * g
        mine = aligned(k, g)
        whole = aligned(m >> log2(shards), CLUS)
        top, delta = [], []
        for j in range(shards):
            at = (tab[first + j] ^ me) * 2 * shards + tab[cfg["chunks"] + first + j]
            top.append(stats[pl.ds(at, 1), 0:g])
            delta.append(stats[pl.ds(at + shards, 1), 0:g])
        allowed = query_at >= key_at + rank
        p = jnp.exp(jnp.where(allowed, s_ref[mine, :] - jnp.concatenate(top, axis=1), NEG))
        ds = p * (dp_ref[mine, :] - jnp.concatenate(delta, axis=1)) * scale
        outs[mine, 0:hd] = dot(ds.astype(BF16), rows_ref[whole, 0:hd]).astype(BF16)
        outs[mine, hd:] = dot(p.astype(BF16), rows_ref[whole, hd:]).astype(BF16)
        return carry

    lax.fori_loop(0, shards, step, 0, unroll=min(shards, 8))
    back = dot(back_ref[...], outs[...]).astype(BF16)
    dk_ref[:, hd:] = back[:, 0:hd]
    dv_ref[:, hd:] = back[:, hd:]
    for copy in copies:
        copy.wait()


def partner(array, axis, mask):
    return lax.ppermute(array, axis, [(i, i ^ mask) for i in range(lax.axis_size(axis))])


def after(arrays, *earlier):
    return lax.optimization_barrier((arrays, earlier))[0]


def on_device(query_rows, key_rows, value_rows, out_grad, members):
    tok, width = query_rows.shape
    assert tok == WINDOW
    hd = width // 2
    shards = lax.axis_size("seq")
    heads = lax.axis_size("head")
    bits = log2(shards)
    me = lax.axis_index("seq")
    per = members.shape[0]
    total = per * shards * heads
    g = CLUS // shards
    cfg = dict(
        shards=shards, heads=heads, tok=tok, hd=hd, per=per, g=g, chunks=total // g, per_row=per // g
    )
    big = 2 if shards <= 8 else 4
    full = shape(tok, width)
    sides = [query_rows, key_rows, value_rows, out_grad]
    evens = list(range(2, shards, 2))

    kv_c, qg_c, kv_w, qg_w, *pieces, both, rim, spread = call(
        functools.partial(payloads, bits, hd),
        [full] * (bits + 3) + [shape(tok, 3 * width), full, shape(shards * heads, per, dtype=jnp.int32)],
        [pltpu.with_memory_space_constraint(x, pltpu.HBM) for x in [members.reshape(1, per)] + sides],
        scratch=[
            pltpu.VMEM((1, per), jnp.int32),
            pltpu.VMEM((shards * heads, per), jnp.int32),
            pltpu.SemaphoreType.DMA((10,)),
        ],
        hbm_outs=(bits + 5,),
        anywhere=(0, 1, 2, 3, 4),
        vmem=6 + bits,
    )
    got = {mask: partner(pieces[mask.bit_length() - 2], "seq", mask) for mask in evens}
    got[1] = partner(both, "seq", 1)
    lists = lax.all_to_all(after(spread, got[1]), ("seq", "head"), 0, 0, tiled=True)
    crossing = [(i, i + 1) for i in range(1, shards - 1, 2)] + [(shards - 1, 0)]
    crossing += [(b, a) for a, b in crossing]
    far = lax.ppermute(after(rim, lists), "seq", crossing)
    for mask in evens:
        got[mask + 1] = partner(after(got[mask], lists), "seq", 1)

    table = 3 * (total // g)
    rows_shape = shape(total, 2 * hd)
    stat = shape(2 * shards, LANES, dtype=F32)
    rows, qg, kv, back, p, ds, st_c, tab = call(
        functools.partial(sort_and_score, cfg),
        [rows_shape, full, full, shape(tok, tok), shape(tok, CLUS), shape(tok, CLUS), stat, shape(table, dtype=jnp.int32)],
        [lists, kv_c, qg_c] + [got[mask] for mask in range(1, shards)],
        scratch=[
            pltpu.SMEM((shards * heads, per), jnp.int32),
            pltpu.SMEM((table,), jnp.int32),
            pltpu.SMEM((shards,), jnp.int32),
            pltpu.SemaphoreType.DMA((2,)),
            pltpu.VMEM((total, LANES), F32),
            pltpu.VMEM((2, tok, tok), BF16),
            pltpu.VMEM((2, tok, 2 * hd), BF16),
        ],
        us=5.0,
        vmem=12 * big,
    )
    tile = 128
    def gather_step(held, bit, *earlier):
        return held, partner(after(held, *earlier), "seq", 1 << bit)

    def joined(held, other):
        rows_of = held.shape[0]
        return call(join, [shape(2 * rows_of, LANES, dtype=F32)], [held, other], vmem=2)[0]

    other, beyond = partner(st_c, "seq", 1), partner(st_c, "seq", 2)
    scored = shape(tok, CLUS, dtype=F32)
    rows, outs, s, dp = call(
        functools.partial(finish_queries, cfg),
        [rows_shape, full, scored, scored],
        [tab, rows, p, ds, qg, kv],
        smem=(0,),
        us=2.0,
        aliases={1: 0},
        vmem=6 * big,
    )
    behind = partner(after(beyond, outs), "seq", 1)
    window = shape(tok, tok + tile)
    longer = shape(2 * tok, hd)
    p_w, ds_w, st_w, kx, vx = call(
        functools.partial(window_scores, tok, hd, tile),
        [window, window, shape(8, tok, dtype=F32), longer, longer],
        [after(kv_w, outs), qg_w, got[1], far],
        us=1.3,
        vmem=8,
    )
    held, other = joined(st_c, other), joined(beyond, after(behind, st_w))
    for bit in range(2, bits):
        held, other = gather_step(joined(held, other), bit)
    st_next = lax.ppermute(st_w, "seq", [((i + 1) % shards, i) for i in range(shards)])
    scores = shape(tok, tok + tile, dtype=F32)
    out_all, dq_all, s_w, dp_w, qx, gx = call(
        functools.partial(query_outputs, tok, hd, tile),
        [full, full, scores, scores, longer, longer],
        [p_w, ds_w, kx, vx, back, outs, kv_w, qg_w, got[1], far],
        us=0.2,
        vmem=12,
    )
    return call(
        functools.partial(key_outputs, cfg, tile),
        [full] * 4,
        [tab, rows, back, s, dp, held, other, out_all, dq_all, s_w, dp_w, qx, gx, st_w, st_next],
        scratch=[
            pltpu.SMEM((table,), jnp.int32),
            pltpu.VMEM((2 * shards * shards, LANES), F32),
            pltpu.VMEM((tok, 2 * hd), BF16),
            pltpu.SemaphoreType.DMA((3,)),
            pltpu.VMEM((8, 2 * tok), F32),
        ],
        hbm_outs=(0, 1),
        us=3.3,
        vmem=5 * big,
    )


def solution(mesh):
    rows = P("seq", "head")
    return jax.shard_map(
        on_device,
        mesh=mesh,
        in_specs=(rows, rows, rows, rows, P(("seq", "head"))),
        out_specs=(rows, rows, rows, rows),
        check_vma=False,
    )
```
